512 devices in a mesh: member: 32 (over z, x), tensor: 16 (over y, core).
Axes of the slice: x: 4, y: 8, z: 8, core: 2. Of those that a mesh axis runs over, the one named last changes fastest.
Arguments:
- query: bfloat16 [16, 32, 8192], P(None, 'member'), may hold values from -106.06602 to 106.06602
- new_kv: bfloat16 [2, 16, 32, 1024], P(None, None, 'member'), may hold values from -20 to 20
- cache: bfloat16 [2, 32, 1024, 1024], P(None, 'member', 'tensor'), may hold values from -6 to 6
- lengths: int32 [32], P('member'), may hold values from 600 to 1024, as said below
- w_out: bfloat16 [8192, 8192], P('tensor', 'member'), may hold values from -0.625 to 0.625
- resid: bfloat16 [16, 32, 8192], P(None, None, 'member'), may hold values from -20 to 20
- norm_gain: float32 [8192], P('member'), may hold values from 0.5 to 1.5
- head: bfloat16 [8192, 65536], P(None, ('member', 'tensor')), may hold values from -0.198873782 to 0.198873782
- noise: float32 [16, 65536], P(None, ('member', 'tensor')), may hold values from -6 to 6
Outputs:
- noisy_scores: float32 [16, 65536], P(None, ('member', 'tensor'))
The draws below stay inside these ranges and needn't reach their ends.
Inputs may be any that keep to these rules, and one draw needn't show every extreme that they name: `lengths`: at least one prompt fills its whole cache, and at least one has the fewest valid positions.
All inputs are finite; a program needn't handle non-finite values.
Results may differ from the reference program's by a relative error of at most 0.025.
Values may be sent and summed in bfloat16 or wider, within the bound.
No kernel may reach another device: no remote copies, remote signals or barrier semaphores. Data moves between devices by JAX's collectives and lax.ppermute only.
A program may use at most 64 MiB of HBM per device.

```python
import jax
import jax.numpy as jnp
from jax import lax

D = 8192
NH = 64
KVH = 8
HD = 128
CTX = 1024
QUERIES = 16
PROMPTS = 32
VOCAB = 65536


def query_field(key):
    key = jax.random.fold_in(key, 102)
    return jnp.clip(jax.random.normal(key, (QUERIES, PROMPTS, NH * HD), jnp.float32), -6.0, 6.0)


def draw_query(key, part):
    field = query_field(key)
    return field.astype(jnp.bfloat16)


def draw_new_kv(key, part):
    field = query_field(key)
    key = jax.random.fold_in(key, 2)
    first, second = jax.random.split(key)
    shape = (QUERIES, PROMPTS, KVH * HD)
    grouped = jnp.mean(field.reshape(QUERIES, PROMPTS, KVH, NH // KVH, HD), axis=3).reshape(shape)
    extra = jnp.clip(jax.random.normal(first, shape, jnp.float32), -6.0, 6.0)
    new_keys = 2.5 * grouped + 0.3 * extra
    new_values = jnp.clip(jax.random.normal(second, shape, jnp.float32), -6.0, 6.0)
    return jnp.stack([new_keys, new_values]).astype(jnp.bfloat16)


def draw_cache(key, part):
    key = jax.random.fold_in(key, 3)
    first, second = jax.random.split(key)
    shape = (PROMPTS, CTX, KVH * HD)
    key_rows = jnp.clip(jax.random.normal(first, shape, jnp.float32), -6.0, 6.0)
    value_rows = jnp.clip(jax.random.normal(second, shape, jnp.float32), -6.0, 6.0)
    return jnp.stack([key_rows, value_rows]).astype(jnp.bfloat16)


def draw_lengths(key, part):
    key = jax.random.fold_in(key, 4)
    first, second, third = jax.random.split(key, 3)
    lowest = CTX * 75 // 128
    drawn = jax.random.randint(first, (PROMPTS,), lowest, CTX + 1, jnp.int32)
    longest = jax.random.randint(second, (), 0, PROMPTS, jnp.int32)
    shortest = (longest + jax.random.randint(third, (), 1, PROMPTS, jnp.int32)) % PROMPTS
    positions = jnp.arange(PROMPTS, dtype=jnp.int32)
    drawn = jnp.where(positions == longest, CTX, drawn)
    drawn = jnp.where(positions == shortest, lowest, drawn)
    return drawn.astype(jnp.int32)


def draw_resid(key, part):
    key = jax.random.fold_in(key, 5)
    first = jax.random.fold_in(key, 0)
    shape = (QUERIES, PROMPTS, D)
    field = 0.5 * jnp.clip(jax.random.normal(first, shape, jnp.float32), -6.0, 6.0)
    return field.astype(jnp.bfloat16)


def draw_head(key, part):
    key = jax.random.fold_in(key, 6)
    width_scale = 3.0 * D ** (-0.5)
    field = width_scale * jnp.clip(jax.random.normal(key, (D, VOCAB), jnp.float32), -6.0, 6.0)
    return field.astype(jnp.bfloat16)


def block_scale(key, extent, cuts, least, top_value):
    gain = 1.0
    for position, shards_of in cuts:
        heights = jax.random.uniform(jax.random.fold_in(jax.random.fold_in(key, 6), position), (shards_of,), jnp.float32, least / len(cuts), top_value / len(cuts))
        gain = gain * jnp.repeat(jnp.exp(heights), extent[position] // shards_of).reshape((-1,) + (1,) * (len(extent) - 1 - position))
    return gain


def gaussian(key, extent, scale, bound, cuts=(), kind=jnp.bfloat16):
    values = jax.random.normal(key, extent, jnp.float32) * scale
    if len(cuts) > 0:
        values = block_scale(key, extent, cuts, -0.22, 0.18) * values
    return jnp.clip(values, min=-bound, max=bound).astype(kind)


def setup_inputs(seed: int = 0) -> dict:
    key_list = jax.random.split(jax.random.key(seed), 10)
    return {
        "query": draw_query(jax.random.fold_in(key_list[9], 71), 0),
        "new_kv": draw_new_kv(jax.random.fold_in(key_list[9], 71), 0),
        "cache": draw_cache(jax.random.fold_in(key_list[9], 71), 0),
        "lengths": draw_lengths(jax.random.fold_in(key_list[9], 71), 0),
        "w_out": gaussian(key_list[4], (NH * HD, D), (4 * (NH * HD) ** -0.5), 0.625, ((0, 16), (1, 32))),
        "resid": draw_resid(jax.random.fold_in(key_list[9], 71), 0),
        "norm_gain": jnp.clip(1.0 + 0.1 * jax.random.normal(key_list[6], (D,), jnp.float32), 0.5, 1.5),
        "head": draw_head(jax.random.fold_in(key_list[9], 71), 0),
        "noise": gaussian(key_list[8], (QUERIES, VOCAB), 0.5, 6.0, ((1, 512),), jnp.float32),
    }


def attend(prompt_item):
    query_rows, new_key, new_value, key_rows, value_rows, length = prompt_item
    group = NH // KVH
    score_scale = HD ** (-0.5)
    grouped = query_rows.astype(jnp.float32).reshape(QUERIES, KVH, group, HD)
    key_block = key_rows.astype(jnp.float32).reshape(CTX, KVH, HD)
    value_block = value_rows.astype(jnp.float32).reshape(CTX, KVH, HD)
    scores = jnp.einsum('qgrd,kgd->qgrk', grouped, key_block) * score_scale
    own_key = new_key.astype(jnp.float32).reshape(QUERIES, KVH, HD)
    own_score = jnp.einsum('qgrd,qgd->qgr', grouped, own_key) * score_scale
    valid_mask = jnp.arange(CTX, dtype=jnp.int32) < length
    scores = jnp.where(valid_mask, scores, -jnp.inf)
    row_top = jnp.maximum(lax.optimization_barrier(jnp.max(scores, axis=-1)), own_score)
    weights = jnp.exp(scores - row_top[..., None])
    own_weight = jnp.exp(own_score - row_top)
    denominator = lax.optimization_barrier(jnp.sum(weights, axis=-1)) + own_weight
    rounded = lax.optimization_barrier(weights.astype(jnp.bfloat16)).astype(jnp.float32)
    own_rounded = lax.optimization_barrier(own_weight.astype(jnp.bfloat16)).astype(jnp.float32)
    own_value = new_value.astype(jnp.float32).reshape(QUERIES, KVH, HD)
    numerator = jnp.einsum('qgrk,kgd->qgrd', rounded, value_block)
    numerator = numerator + own_rounded[..., None] * own_value[:, :, None, :]
    return (numerator / denominator[..., None]).reshape(QUERIES, NH * HD).astype(jnp.bfloat16)

def reference(query, new_kv, cache, lengths, w_out, resid, norm_gain, head, noise):
    items = (jnp.swapaxes(query, 0, 1), jnp.swapaxes(new_kv[0], 0, 1), jnp.swapaxes(new_kv[1], 0, 1), cache[0], cache[1], lengths)
    attended = jnp.swapaxes(lax.map(attend, items), 0, 1)
    projected = jnp.dot(attended.reshape(QUERIES * PROMPTS, NH * HD), w_out, preferred_element_type=jnp.float32)
    hidden = (resid.astype(jnp.float32) + projected.reshape(QUERIES, PROMPTS, D)).astype(jnp.bfloat16)
    hidden_f32 = hidden.astype(jnp.float32)
    mean_square = lax.optimization_barrier(jnp.mean(hidden_f32 * hidden_f32, axis=-1))
    normed = (hidden_f32 * lax.rsqrt(mean_square + 1e-05)[..., None] * norm_gain).astype(jnp.bfloat16)

    def vocab_row(normed_rows):
        logits = jnp.dot(normed_rows, head, preferred_element_type=jnp.float32)
        logit_top = lax.optimization_barrier(jnp.max(logits, axis=-1))
        exp_terms = jnp.exp(logits - logit_top[:, None])
        probabilities = exp_terms / lax.optimization_barrier(jnp.sum(exp_terms, axis=-1))[:, None]
        return lax.optimization_barrier(jnp.mean(probabilities, axis=0))
    averaged = lax.map(vocab_row, normed)
    return jnp.log(VOCAB * averaged) + noise
```

```python
import functools

import jax
import jax.numpy as jnp
from jax import lax
from jax.experimental import pallas as pl
from jax.experimental.pallas import tpu as pltpu
from jax.sharding import Mesh
from jax.sharding import PartitionSpec as P

NZ, NX, NY, NC = 8, 4, 8, 2
MEMBER = ("z", "x")
TENSOR = ("y", "c")

D = 8192
KVH = 8
GROUP = 8
HD = 128
QUERIES = 16
PROMPTS = 32
VOCAB = 65536
ROWS = PROMPTS * QUERIES
CACHE_ROWS = 64
LOW = -1e30

BF16 = jnp.bfloat16
F32 = jnp.float32


def call(body, out_shape, operands, spaces=None):
    vmem = pl.BlockSpec(memory_space=pltpu.VMEM)
    smem = pl.BlockSpec(memory_space=pltpu.SMEM)
    spaces = spaces or "v" * len(operands)
    return pl.pallas_call(
        body,
        out_shape=out_shape,
        in_specs=[smem if s == "s" else vmem for s in spaces],
        out_specs=jax.tree.map(lambda _: vmem, out_shape),
    )(*operands)


def shape(dims, dtype=BF16):
    return jax.ShapeDtypeStruct(dims, dtype)


def split_pair(value):
    high = value.astype(BF16).astype(F32)
    return high, value - high


def diagonal(rows):
    return lax.broadcasted_iota(jnp.int32, (rows, 128), 0) == lax.broadcasted_iota(
        jnp.int32, (rows, 128), 1
    )


def to_row(column):
    return jnp.sum(jnp.where(diagonal(column.shape[0]), column, 0.0), axis=0, keepdims=True)


def to_column(row):
    return jnp.sum(jnp.where(diagonal(128), row, 0.0), axis=1, keepdims=True)


def attend_kernel(length_ref, query_ref, new_ref, cache_ref, out_ref):
    tensor_index = lax.axis_index("y") * NC + lax.axis_index("c")
    valid_rows = length_ref[0] - tensor_index * CACHE_ROWS
    positions = CACHE_ROWS + QUERIES
    row = lax.broadcasted_iota(jnp.int32, (positions, 128), 0)
    lane = lax.broadcasted_iota(jnp.int32, (positions, 128), 1)
    own_from = jnp.where(tensor_index == 0, CACHE_ROWS, positions)
    valid = ((row < CACHE_ROWS) & (row < valid_rows)) | (
        (row >= own_from) & (row - CACHE_ROWS == lane % QUERIES)
    )
    stat_row = lax.broadcasted_iota(jnp.int32, (16, 128), 0)
    for g in range(KVH):
        columns = slice(g * HD, (g + 1) * HD)
        heads = [
            query_ref[:, (g * GROUP + r) * HD : (g * GROUP + r + 1) * HD] for r in range(GROUP)
        ]
        rows = jnp.concatenate(heads, axis=0)
        keys = jnp.concatenate([cache_ref[0, :, columns], new_ref[0, :, columns]], axis=0)
        values = jnp.concatenate([cache_ref[1, :, columns], new_ref[1, :, columns]], axis=0)
        scores = lax.dot_general(
            keys, rows, (((1,), (1,)), ((), ())), preferred_element_type=F32
        ) * HD ** (-0.5)
        scores = jnp.where(valid, scores, LOW)
        top = jnp.max(scores, axis=0, keepdims=True).astype(BF16).astype(F32)
        weights = jnp.where(valid, jnp.exp(scores - top), 0.0)
        high, low = split_pair(jnp.sum(weights, axis=0, keepdims=True))
        totals = lax.dot_general(
            weights.astype(BF16), values, (((0,), (0,)), ((), ())), preferred_element_type=F32
        ).astype(BF16)
        stats = jnp.where(
            stat_row == 0,
            top,
            jnp.where(stat_row == 1, high, jnp.where(stat_row == 2, low, 0.0)),
        ).astype(BF16)
        for half in range(2):
            out_ref[2 * g + half, 0:64, :] = totals[64 * half : 64 * half + 64]
            out_ref[2 * g + half, 64:80, :] = stats


def combine_kernel(parts_ref, out_ref):
    core = lax.axis_index("c")
    stats = parts_ref[:, 64:80, :].astype(F32)
    tops, totals = stats[:, 0, :], stats[:, 1, :] + stats[:, 2, :]
    weight = jnp.exp(tops - jnp.max(tops, axis=0, keepdims=True))
    scale = weight / jnp.sum(weight * totals, axis=0, keepdims=True)
    scale = jnp.concatenate([scale, jnp.zeros((112, 128), F32)], axis=0).T
    scale = jnp.where(core == 1, scale[64:, :], scale[:64, :])
    attended = jnp.zeros((64, 128), F32)
    for source in range(NY * NC):
        attended += scale[:, source : source + 1] * parts_ref[source, 0:64, :].astype(F32)
    attended = attended.astype(BF16)
    for target in range(NZ * NX):
        out_ref[target] = attended


def project_kernel(attended_ref, weight_ref, out_ref):
    features = jnp.concatenate(
        [attended_ref[:, 16 * r : 16 * r + 16, :].reshape(ROWS, HD) for r in range(4)], axis=1
    )
    partial = jnp.dot(features, weight_ref[...], preferred_element_type=F32).astype(BF16)
    for y in range(NY):
        for c in range(NC):
            out_ref[NC * y + c] = partial[64 * y : 64 * y + 64, 128 * c : 128 * c + 128]


def residual_kernel(parts_ref, resid_ref, gain_ref, out_ref):
    core = lax.axis_index("c")
    hidden = resid_ref[...].astype(F32)
    projected = parts_ref[0].astype(F32)
    for source in range(1, NY * NC):
        projected += parts_ref[source].astype(F32)
    hidden += projected
    gain = jnp.where(core == 1, gain_ref[1:2, :], gain_ref[0:1, :])
    high, low = split_pair(to_row(jnp.sum(hidden * hidden, axis=1, keepdims=True)))
    stat_row = lax.broadcasted_iota(jnp.int32, (16, 128), 0)
    stats = jnp.where(stat_row == 0, high, jnp.where(stat_row == 1, low, 0.0)).astype(BF16)
    scaled = (hidden * gain).astype(BF16)
    for target in range(out_ref.shape[0]):
        out_ref[target, 0:64, :] = scaled
        out_ref[target, 64:80, :] = stats


def relay_kernel(parts_ref, out_ref):
    total = jnp.zeros((1, 128), F32)
    for z in range(NZ):
        total += jnp.sum(parts_ref[z, 64:80, :].astype(F32), axis=0, keepdims=True)
    high, low = split_pair(total)
    stat_row = lax.broadcasted_iota(jnp.int32, (16, 128), 0)
    stats = jnp.where(stat_row == 0, high, jnp.where(stat_row == 1, low, 0.0)).astype(BF16)
    for y in range(NY):
        for z in range(NZ):
            out_ref[y, 64 * z : 64 * z + 64, :] = parts_ref[z, 0:64, :]
        out_ref[y, 512:528, :] = stats


def head_kernel(rows_ref, head_ref, out_ref):
    features = jnp.concatenate(
        [
            jnp.concatenate([rows_ref[y, 64 * z : 64 * z + 64, :] for z in range(NZ)], axis=1)
            for y in range(NY)
        ],
        axis=0,
    )
    stat_row = lax.broadcasted_iota(jnp.int32, (16, 128), 0)
    stats = jnp.zeros((16, 128), F32)
    for y in range(NY):
        pair = rows_ref[y, 512:528, :].astype(F32)
        stats = jnp.where(
            stat_row == y, pair[0:1], jnp.where(stat_row == NY + y, pair[1:2], stats)
        )
    stats = stats.astype(BF16)
    for pair in range(4):
        block = jnp.concatenate(
            [head_ref[2 * pair + k].reshape(NZ * 128, 128) for k in range(2)], axis=1
        )
        partial = jnp.dot(features, block, preferred_element_type=F32).astype(BF16)
        for k in range(2):
            out_ref[2 * pair + k, 0:ROWS, :] = partial[:, 128 * k : 128 * k + 128]
            out_ref[2 * pair + k, ROWS : ROWS + 16, :] = stats


def logit_kernel(parts_ref, logits_ref, out_ref):
    stats = parts_ref[0, ROWS : ROWS + 16, :].astype(F32)
    for source in range(1, NX * NC):
        stats += parts_ref[source, ROWS : ROWS + 16, :].astype(F32)
    factor = lax.rsqrt((stats[0:NY] + stats[NY:]) / D + 1e-05)
    tops, totals = [], []
    for block in range(4):
        rows = slice(128 * block, 128 * block + 128)
        logits = parts_ref[0, rows, :].astype(F32)
        for source in range(1, NX * NC):
            logits += parts_ref[source, rows, :].astype(F32)
        column = jnp.concatenate(
            [to_column(factor[2 * block + k : 2 * block + k + 1])[0:64] for k in range(2)], axis=0
        )
        logits = logits * column
        logits_ref[rows, :] = logits
        top = jnp.max(logits, axis=1, keepdims=True)
        tops.append(to_row(top))
        totals.append(to_row(jnp.sum(jnp.exp(logits - top), axis=1, keepdims=True)))
    packed = jnp.concatenate(tops + totals, axis=0)
    for target in range(NY * NC):
        out_ref[target] = packed


def merge_stats(parts):
    tops = parts[:, 0:4, :]
    top = jnp.max(tops, axis=0)
    total = jnp.sum(jnp.exp(tops - top[None]) * parts[:, 4:8, :], axis=0)
    return top, total


def merge_kernel(parts_ref, out_ref):
    top, total = merge_stats(parts_ref[...])
    packed = jnp.concatenate([top, total], axis=0)
    for target in range(NZ * NX):
        out_ref[target] = packed


def vote_kernel(parts_ref, logits_ref, noise_ref, out_ref):
    top, total = merge_stats(parts_ref[...])
    averaged = jnp.zeros((QUERIES, 128), F32)
    for block in range(4):
        mass = jnp.exp(
            logits_ref[128 * block : 128 * block + 128, :] - to_column(top[block : block + 1])
        ) / to_column(total[block : block + 1])
        averaged += jnp.sum(mass.reshape(8, QUERIES, 128), axis=0)
    out_ref[...] = jnp.log(VOCAB * (averaged / PROMPTS)) + noise_ref[...]


def exchange(array, axes):
    return lax.all_to_all(array, axes, 0, 0, tiled=True)


def on_device(query, new_kv, cache, lengths, w_out, resid, norm_gain, head, noise):
    y, c = lax.axis_index("y"), lax.axis_index("c")
    head_rows = lax.all_to_all(
        head.reshape(NZ, NX * NC, 128, 128), ("x", "c"), split_axis=1, concat_axis=0
    )
    resid_mine = jnp.swapaxes(
        lax.dynamic_slice(resid, (0, 4 * y, 128 * c), (QUERIES, 4, 128)), 0, 1
    ).reshape(64, 128)

    parts = call(
        attend_kernel,
        shape((NY * NC, 80, 128)),
        (lengths, query[:, 0, :], new_kv[:, :, 0, :], cache[:, 0]),
        "svvv",
    )
    parts = exchange(parts, TENSOR)
    attended = call(combine_kernel, shape((NZ * NX, 64, 128)), (parts,))
    attended = exchange(attended, MEMBER)
    partial = call(project_kernel, shape((NY * NC, 64, 128)), (attended, w_out))
    partial = exchange(partial, TENSOR)
    hidden = call(
        residual_kernel, shape((NZ, 80, 128)), (partial, resid_mine, norm_gain.reshape(2, 128))
    )
    hidden = exchange(hidden, ("z",))
    rows = call(relay_kernel, shape((NY, 528, 128)), (hidden,))
    rows = exchange(rows, ("y",))
    logits = call(head_kernel, shape((NX * NC, ROWS + 16, 128)), (rows, head_rows))
    logits = exchange(logits, ("x", "c"))
    logits, stats = call(
        logit_kernel, (shape((ROWS, 128), F32), shape((NY * NC, 8, 128), F32)), (logits,)
    )
    stats = exchange(stats, TENSOR)
    stats = call(merge_kernel, shape((NZ * NX, 8, 128), F32), (stats,))
    stats = exchange(stats, MEMBER)
    return call(vote_kernel, shape((QUERIES, 128), F32), (stats, logits, noise))


def solution(mesh):
    torus = Mesh(mesh.devices.reshape(NZ, NX, NY, NC), MEMBER + TENSOR)
    placed = (
        P(None, MEMBER, None),
        P(None, None, MEMBER, None),
        P(None, MEMBER, TENSOR, None),
        P(MEMBER),
        P(TENSOR, MEMBER),
        P(None, None, MEMBER),
        P(MEMBER),
        P(None, MEMBER + TENSOR),
        P(None, MEMBER + TENSOR),
    )
    return jax.shard_map(
        on_device,
        mesh=torus,
        in_specs=placed,
        out_specs=P(None, MEMBER + TENSOR),
        check_vma=False,
    )
```

```python
import jax
import jax.numpy as jnp
from jax import lax
from jax.experimental import pallas as pl
from jax.experimental.pallas import tpu as pltpu
from jax.sharding import Mesh
from jax.sharding import PartitionSpec as P

NZ, NX, NY, NC = 8, 4, 8, 2
MEMBER = ("z", "x")
TENSOR = ("y", "c")

D = 8192
KVH = 8
GROUP = 8
HD = 128
QUERIES = 16
PROMPTS = 32
VOCAB = 65536
ROWS = PROMPTS * QUERIES
CACHE_ROWS = 64
LOW = -1e30

BF16 = jnp.bfloat16
F32 = jnp.float32


def call(body, out_shape, operands, spaces=None, scratch=(), mebibytes=8):
    vmem = pl.BlockSpec(memory_space=pltpu.VMEM)
    kinds = {
        "v": vmem,
        "s": pl.BlockSpec(memory_space=pltpu.SMEM),
        "a": pl.BlockSpec(memory_space=pltpu.HBM),
        "w": pl.BlockSpec(memory_space=pl.ANY),
    }
    return pl.pallas_call(
        body,
        out_shape=out_shape,
        in_specs=[kinds[s] for s in spaces or "v" * len(operands)],
        out_specs=jax.tree.map(lambda _: vmem, out_shape),
        scratch_shapes=scratch,
        compiler_params=pltpu.CompilerParams(vmem_limit_bytes=mebibytes * 2**20),
    )(*operands)


def shape(dims, dtype=BF16):
    return jax.ShapeDtypeStruct(dims, dtype)


def split_pair(value):
    high = value.astype(BF16).astype(F32)
    return high, value - high


def diagonal(rows):
    return lax.broadcasted_iota(jnp.int32, (rows, 128), 0) == lax.broadcasted_iota(
        jnp.int32, (rows, 128), 1
    )


def to_row(column):
    return jnp.sum(jnp.where(diagonal(column.shape[0]), column, 0.0), axis=0, keepdims=True)


def to_column(row):
    return jnp.sum(jnp.where(diagonal(128), row, 0.0), axis=1, keepdims=True)


def attend_kernel(length_ref, *refs):
    sources, out_ref, buffers, semaphores = refs[:3], refs[3], refs[4:7], refs[7]
    copies = [
        pltpu.make_async_copy(source, buffer, semaphores.at[i])
        for i, (source, buffer) in enumerate(zip(sources, buffers))
    ]
    for copy in copies:
        copy.start()
    query_ref, new_ref, cache_ref = buffers
    tensor_index = lax.axis_index("y") * NC + lax.axis_index("c")
    valid_rows = length_ref[0] - tensor_index * CACHE_ROWS
    positions = CACHE_ROWS + QUERIES
    row = lax.broadcasted_iota(jnp.int32, (positions, 128), 0)
    lane = lax.broadcasted_iota(jnp.int32, (positions, 128), 1)
    own_from = jnp.where(tensor_index == 0, CACHE_ROWS, positions)
    valid = ((row < CACHE_ROWS) & (row < valid_rows)) | (
        (row >= own_from) & (row - CACHE_ROWS == lane % QUERIES)
    )
    stat_row = lax.broadcasted_iota(jnp.int32, (16, 128), 0)
    for copy in copies:
        copy.wait()
    for g in range(KVH):
        columns = slice(g * HD, (g + 1) * HD)
        heads = [
            query_ref[:, (g * GROUP + r) * HD : (g * GROUP + r + 1) * HD] for r in range(GROUP)
        ]
        rows = jnp.concatenate(heads, axis=0)
        keys = jnp.concatenate([cache_ref[0, :, columns], new_ref[0, :, columns]], axis=0)
        values = jnp.concatenate([cache_ref[1, :, columns], new_ref[1, :, columns]], axis=0)
        scores = lax.dot_general(
            keys, rows, (((1,), (1,)), ((), ())), preferred_element_type=F32
        ) * HD ** (-0.5)
        scores = jnp.where(valid, scores, LOW)
        top = jnp.max(scores, axis=0, keepdims=True).astype(BF16).astype(F32)
        weights = jnp.where(valid, jnp.exp(scores - top), 0.0)
        high, low = split_pair(jnp.sum(weights, axis=0, keepdims=True))
        totals = lax.dot_general(
            weights.astype(BF16), values, (((0,), (0,)), ((), ())), preferred_element_type=F32
        ).astype(BF16)
        stats = jnp.where(
            stat_row == 0,
            top,
            jnp.where(stat_row == 1, high, jnp.where(stat_row == 2, low, 0.0)),
        ).astype(BF16)
        for half in range(2):
            out_ref[2 * g + half, 0:64, :] = totals[64 * half : 64 * half + 64]
            out_ref[2 * g + half, 64:80, :] = stats


def combine_kernel(parts_ref, out_ref):
    core = lax.axis_index("c")
    stats = parts_ref[:, 64:80, :].astype(F32)
    tops, totals = stats[:, 0, :], stats[:, 1, :] + stats[:, 2, :]
    weight = jnp.exp(tops - jnp.max(tops, axis=0, keepdims=True))
    scale = weight / jnp.sum(weight * totals, axis=0, keepdims=True)
    scale = jnp.concatenate([scale, jnp.zeros((112, 128), F32)], axis=0).T
    scale = jnp.where(core == 1, scale[64:, :], scale[:64, :])
    attended = jnp.zeros((64, 128), F32)
    for source in range(NY * NC):
        attended += scale[:, source : source + 1] * parts_ref[source, 0:64, :].astype(F32)
    attended = attended.astype(BF16)
    for target in range(NZ * NX):
        out_ref[target] = attended


def project_kernel(attended_ref, weight_ref, out_ref):
    features = jnp.concatenate(
        [attended_ref[:, 16 * r : 16 * r + 16, :].reshape(ROWS, HD) for r in range(4)], axis=1
    )
    partial = jnp.dot(features, weight_ref[...], preferred_element_type=F32).astype(BF16)
    for y in range(NY):
        for c in range(NC):
            out_ref[NC * y + c] = partial[64 * y : 64 * y + 64, 128 * c : 128 * c + 128]


def residual_kernel(parts_ref, resid_ref, gain_ref, out_ref):
    core = lax.axis_index("c")
    hidden = resid_ref[...].astype(F32)
    projected = parts_ref[0].astype(F32)
    for source in range(1, NY * NC):
        projected += parts_ref[source].astype(F32)
    hidden += projected
    gain = jnp.where(core == 1, gain_ref[1:2, :], gain_ref[0:1, :])
    high, low = split_pair(to_row(jnp.sum(hidden * hidden, axis=1, keepdims=True)))
    stat_row = lax.broadcasted_iota(jnp.int32, (8, 128), 0)
    stats = jnp.where(stat_row == 0, high, jnp.where(stat_row == 1, low, 0.0)).astype(BF16)
    scaled = (hidden * gain).astype(BF16)
    for target in range(NZ * NY):
        out_ref[target, 0:64, :] = scaled
        out_ref[target, 64:72, :] = stats


def gathered(ref):
    return jnp.concatenate(
        [
            jnp.concatenate([ref[NY * z + y, 0:64, :] for z in range(NZ)], axis=1)
            for y in range(NY)
        ],
        axis=0,
    )


def square_totals(ref):
    return [sum(ref[NY * z + y, 64:72, :].astype(F32) for z in range(NZ)) for y in range(NY)]


def head_block(refs, start):
    rows = pl.ds(pl.multiple_of(start, 128), 128)
    return jnp.concatenate([ref[:, rows, :].reshape(NZ * 128, 128) for ref in refs], axis=1)


def near_kernel(mine_ref, head_ref, *refs):
    swapped_refs, (out_ref, block_ref, semaphore) = refs[:3], refs[3:]
    fetch = pltpu.make_async_copy(head_ref.at[:, lax.axis_index("x")], block_ref, semaphore)
    fetch.start()
    start = lax.axis_index("c") * 128
    mine = gathered(mine_ref)
    fetch.wait()
    blocks = (block_ref,) + swapped_refs
    for pair in range(NX // 2):
        out_ref[pair] = jnp.dot(
            mine, head_block(blocks[2 * pair : 2 * pair + 2], start), preferred_element_type=F32
        )


def far_kernel(mine_ref, other_ref, near_ref, head_ref, *refs):
    swapped_refs, (out_ref, block_ref, semaphore) = refs[:3], refs[3:]
    x = lax.axis_index("x")
    fetch = pltpu.make_async_copy(head_ref.at[:, x], block_ref, semaphore)
    fetch.start()
    start = (1 - lax.axis_index("c")) * 128
    stat_row = lax.broadcasted_iota(jnp.int32, (16, 128), 0)
    stats = jnp.zeros((16, 128), F32)
    for y, (mine, other) in enumerate(zip(square_totals(mine_ref), square_totals(other_ref))):
        high, low = split_pair(jnp.sum(mine + other, axis=0, keepdims=True))
        stats = jnp.where(stat_row == y, high, jnp.where(stat_row == NY + y, low, stats))
    stats = stats.astype(BF16)
    other = gathered(other_ref)
    fetch.wait()
    blocks = (block_ref,) + swapped_refs
    for pair in range(NX // 2):
        partial = near_ref[pair] + jnp.dot(
            other, head_block(blocks[2 * pair : 2 * pair + 2], start), preferred_element_type=F32
        )
        partial = partial.astype(BF16)
        for k in range(2):
            target = lax.rem(x + NX - (2 * pair + k), NX)
            out_ref[target, 0:ROWS, :] = partial[:, 128 * k : 128 * k + 128]
            out_ref[target, ROWS : ROWS + 16, :] = stats


def logit_kernel(parts_ref, logits_ref, out_ref):
    stats = parts_ref[0, ROWS : ROWS + 16, :].astype(F32)
    for source in range(1, NX):
        stats += parts_ref[source, ROWS : ROWS + 16, :].astype(F32)
    factor = lax.rsqrt((stats[0:NY] + stats[NY:]) / D + 1e-05)
    tops, totals = [], []
    for block in range(4):
        rows = slice(128 * block, 128 * block + 128)
        logits = parts_ref[0, rows, :].astype(F32)
        for source in range(1, NX):
            logits += parts_ref[source, rows, :].astype(F32)
        column = jnp.concatenate(
            [to_column(factor[2 * block + k : 2 * block + k + 1])[0:64] for k in range(2)], axis=0
        )
        logits = logits * column
        logits_ref[rows, :] = logits
        top = jnp.max(logits, axis=1, keepdims=True)
        tops.append(to_row(top))
        totals.append(to_row(jnp.sum(jnp.exp(logits - top), axis=1, keepdims=True)))
    packed = jnp.concatenate(tops + totals, axis=0)
    for target in range(NY * NC):
        out_ref[target] = packed


def merge_stats(parts):
    tops = parts[:, 0:4, :]
    top = jnp.max(tops, axis=0)
    total = jnp.sum(jnp.exp(tops - top[None]) * parts[:, 4:8, :], axis=0)
    return top, total


def merge_kernel(parts_ref, out_ref):
    top, total = merge_stats(parts_ref[...])
    packed = jnp.concatenate([top, total], axis=0)
    for target in range(NZ * NX):
        out_ref[target] = packed


def vote_kernel(parts_ref, logits_ref, noise_ref, out_ref):
    top, total = merge_stats(parts_ref[...])
    averaged = jnp.zeros((QUERIES, 128), F32)
    for block in range(4):
        mass = jnp.exp(
            logits_ref[128 * block : 128 * block + 128, :] - to_column(top[block : block + 1])
        ) / to_column(total[block : block + 1])
        averaged += jnp.sum(mass.reshape(8, QUERIES, 128), axis=0)
    out_ref[...] = jnp.log(VOCAB * (averaged / PROMPTS)) + noise_ref[...]


def exchange(array, axes):
    return lax.all_to_all(array, axes, 0, 0, tiled=True)


def on_device(query, new_kv, cache, lengths, w_out, resid, norm_gain, head, noise):
    y, c = lax.axis_index("y"), lax.axis_index("c")
    x = lax.axis_index("x")
    blocks = head.reshape(NZ, NX, 256, 128)
    swapped = [
        lax.ppermute(
            lax.dynamic_index_in_dim(blocks, (x + k) % NX, 1, keepdims=False),
            "x",
            [(i, (i + k) % NX) for i in range(NX)],
        )
        for k in range(1, NX)
    ]
    resid_mine = jnp.swapaxes(
        lax.dynamic_slice(resid, (0, 4 * y, 128 * c), (QUERIES, 4, 128)), 0, 1
    ).reshape(64, 128)

    parts = call(
        attend_kernel,
        shape((NY * NC, 80, 128)),
        (lengths, query[:, 0, :], new_kv[:, :, 0, :], cache[:, 0]),
        "saaa",
        (
            pltpu.VMEM((QUERIES, D), BF16),
            pltpu.VMEM((2, QUERIES, KVH * HD), BF16),
            pltpu.VMEM((2, CACHE_ROWS, KVH * HD), BF16),
            pltpu.SemaphoreType.DMA((3,)),
        ),
    )
    parts = exchange(parts, TENSOR)
    attended = call(combine_kernel, shape((NZ * NX, 64, 128)), (parts,))
    attended = exchange(attended, MEMBER)
    partial = call(project_kernel, shape((NY * NC, 64, 128)), (attended, w_out))
    partial = exchange(partial, TENSOR)
    hidden = call(
        residual_kernel,
        shape((NZ * NY, 72, 128)),
        (partial, resid_mine, norm_gain.reshape(2, 128)),
    )
    mine = exchange(hidden, ("z", "y"))
    mine, *_ = lax.optimization_barrier((mine, *swapped))
    other = lax.ppermute(mine, "c", [(0, 1), (1, 0)])
    scratch = (pltpu.VMEM((NZ, 256, 128), BF16), pltpu.SemaphoreType.DMA)
    near = call(
        near_kernel,
        shape((NX // 2, ROWS, 256), F32),
        (mine, blocks, *swapped),
        "vavvv",
        scratch,
        12,
    )
    logits = call(
        far_kernel,
        shape((NX, ROWS + 16, 128)),
        (mine, other, near, blocks, *swapped),
        "vvvavvv",
        scratch,
        12,
    )
    logits = exchange(logits, ("x",))
    logits, stats = call(
        logit_kernel, (shape((ROWS, 128), F32), shape((NY * NC, 8, 128), F32)), (logits,)
    )
    stats = exchange(stats, TENSOR)
    stats = call(merge_kernel, shape((NZ * NX, 8, 128), F32), (stats,))
    stats = exchange(stats, MEMBER)
    return call(vote_kernel, shape((QUERIES, 128), F32), (stats, logits, noise))


def solution(mesh):
    torus = Mesh(mesh.devices.reshape(NZ, NX, NY, NC), MEMBER + TENSOR)
    placed = (
        P(None, MEMBER, None),
        P(None, None, MEMBER, None),
        P(None, MEMBER, TENSOR, None),
        P(MEMBER),
        P(TENSOR, MEMBER),
        P(None, None, MEMBER),
        P(MEMBER),
        P(None, MEMBER + TENSOR),
        P(None, MEMBER + TENSOR),
    )
    return jax.shard_map(
        on_device,
        mesh=torus,
        in_specs=placed,
        out_specs=P(None, MEMBER + TENSOR),
        check_vma=False,
    )
```

```python
import jax
import jax.numpy as jnp
from jax import lax
from jax.experimental import pallas as pl
from jax.experimental.pallas import tpu as pltpu
from jax.sharding import Mesh
from jax.sharding import PartitionSpec as P

NZ, NX, NY, NC = 8, 4, 8, 2
MEMBER = ("z", "x")
TENSOR = ("y", "c")

D = 8192
KVH = 8
GROUP = 8
HD = 128
QUERIES = 16
PROMPTS = 32
VOCAB = 65536
ROWS = PROMPTS * QUERIES
CACHE_ROWS = 64
LOW = -1e30

BF16 = jnp.bfloat16
F32 = jnp.float32


def call(body, out_shape, operands, spaces=None, scratch=(), mebibytes=8):
    vmem = pl.BlockSpec(memory_space=pltpu.VMEM)
    kinds = {
        "v": vmem,
        "s": pl.BlockSpec(memory_space=pltpu.SMEM),
        "a": pl.BlockSpec(memory_space=pltpu.HBM),
        "w": pl.BlockSpec(memory_space=pl.ANY),
    }
    return pl.pallas_call(
        body,
        out_shape=out_shape,
        in_specs=[kinds[s] for s in spaces or "v" * len(operands)],
        out_specs=jax.tree.map(lambda _: vmem, out_shape),
        scratch_shapes=scratch,
        compiler_params=pltpu.CompilerParams(vmem_limit_bytes=mebibytes * 2**20),
    )(*operands)


def shape(dims, dtype=BF16):
    return jax.ShapeDtypeStruct(dims, dtype)


def split_pair(value):
    high = value.astype(BF16).astype(F32)
    return high, value - high


def diagonal(rows):
    return lax.broadcasted_iota(jnp.int32, (rows, 128), 0) == lax.broadcasted_iota(
        jnp.int32, (rows, 128), 1
    )


def to_row(column):
    return jnp.sum(jnp.where(diagonal(column.shape[0]), column, 0.0), axis=0, keepdims=True)


def to_column(row):
    return jnp.sum(jnp.where(diagonal(128), row, 0.0), axis=1, keepdims=True)


def attend_kernel(length_ref, *refs):
    sources, out_ref, buffers, semaphores = refs[:3], refs[3], refs[4:7], refs[7]
    copies = [
        pltpu.make_async_copy(source, buffer, semaphores.at[i])
        for i, (source, buffer) in enumerate(zip(sources, buffers))
    ]
    for copy in copies:
        copy.start()
    query_ref, new_ref, cache_ref = buffers
    tensor_index = lax.axis_index("y") * NC + lax.axis_index("c")
    valid_rows = length_ref[0] - tensor_index * CACHE_ROWS
    positions = CACHE_ROWS + QUERIES
    row = lax.broadcasted_iota(jnp.int32, (positions, 128), 0)
    lane = lax.broadcasted_iota(jnp.int32, (positions, 128), 1)
    own_from = jnp.where(tensor_index == 0, CACHE_ROWS, positions)
    valid = ((row < CACHE_ROWS) & (row < valid_rows)) | (
        (row >= own_from) & (row - CACHE_ROWS == lane % QUERIES)
    )
    stat_row = lax.broadcasted_iota(jnp.int32, (8, 128), 0)
    for copy in copies:
        copy.wait()
    for g in range(KVH):
        columns = slice(g * HD, (g + 1) * HD)
        heads = [
            query_ref[:, (g * GROUP + r) * HD : (g * GROUP + r + 1) * HD] for r in range(GROUP)
        ]
        rows = jnp.concatenate(heads, axis=0)
        keys = jnp.concatenate([cache_ref[0, :, columns], new_ref[0, :, columns]], axis=0)
        values = jnp.concatenate([cache_ref[1, :, columns], new_ref[1, :, columns]], axis=0)
        scores = lax.dot_general(
            keys, rows, (((1,), (1,)), ((), ())), preferred_element_type=F32
        ) * HD ** (-0.5)
        scores = jnp.where(valid, scores, LOW)
        top = jnp.max(scores, axis=0, keepdims=True).astype(BF16).astype(F32)
        weights = jnp.where(valid, jnp.exp(scores - top), 0.0)
        high, low = split_pair(jnp.sum(weights, axis=0, keepdims=True))
        totals = lax.dot_general(
            weights.astype(BF16), values, (((0,), (0,)), ((), ())), preferred_element_type=F32
        ).astype(BF16)
        stats = jnp.where(
            stat_row == 0,
            top,
            jnp.where(stat_row == 1, high, jnp.where(stat_row == 2, low, 0.0)),
        ).astype(BF16)
        for half in range(2):
            out_ref[NY * half + g, 0:64, :] = totals[64 * half : 64 * half + 64]
            out_ref[NY * half + g, 64:72, :] = stats


def combine_kernel(parts_ref, out_ref):
    core = lax.axis_index("c")
    stats = parts_ref[:, 64:72, :].astype(F32)
    tops, totals = stats[:, 0, :], stats[:, 1, :] + stats[:, 2, :]
    weight = jnp.exp(tops - jnp.max(tops, axis=0, keepdims=True))
    scale = weight / jnp.sum(weight * totals, axis=0, keepdims=True)
    scale = jnp.concatenate([scale, jnp.zeros((112, 128), F32)], axis=0).T
    scale = jnp.where(core == 1, scale[64:, :], scale[:64, :])
    attended = jnp.zeros((64, 128), F32)
    for source in range(NY * NC):
        attended += scale[:, source : source + 1] * parts_ref[source, 0:64, :].astype(F32)
    attended = attended.astype(BF16)
    for target in range(NZ * NX):
        out_ref[target] = attended


def project_kernel(attended_ref, weight_ref, out_ref):
    features = jnp.concatenate(
        [attended_ref[:, 16 * r : 16 * r + 16, :].reshape(ROWS, HD) for r in range(4)], axis=1
    )
    partial = jnp.dot(features, weight_ref[...], preferred_element_type=F32).astype(BF16)
    for y in range(NY):
        rows = jnp.concatenate(
            [partial[16 * (NZ * x + y) : 16 * (NZ * x + y) + 16] for x in range(NX)], axis=0
        )
        for c in range(NC):
            out_ref[NY * c + y] = rows[:, 128 * c : 128 * c + 128]


def residual_kernel(parts_ref, resid_ref, gain_ref, out_ref):
    core = lax.axis_index("c")
    hidden = resid_ref[...].astype(F32)
    projected = parts_ref[0].astype(F32)
    for source in range(1, NY * NC):
        projected += parts_ref[source].astype(F32)
    hidden += projected
    gain = jnp.where(core == 1, gain_ref[1:2, :], gain_ref[0:1, :])
    high, low = split_pair(to_row(jnp.sum(hidden * hidden, axis=1, keepdims=True)))
    stat_row = lax.broadcasted_iota(jnp.int32, (8, 128), 0)
    stats = jnp.where(stat_row == 0, high, jnp.where(stat_row == 1, low, 0.0)).astype(BF16)
    scaled = (hidden * gain).astype(BF16)
    for target in range(NZ * NY):
        out_ref[target, 0:64, :] = scaled
        out_ref[target, 64:72, :] = stats


def gathered(ref):
    return jnp.concatenate(
        [
            jnp.concatenate([ref[NZ * y + z, 0:64, :] for z in range(NZ)], axis=1)
            for y in range(NY)
        ],
        axis=0,
    )


def square_totals(ref):
    return [sum(ref[NZ * y + z, 64:72, :].astype(F32) for z in range(NZ)) for y in range(NY)]


def head_block(refs, start):
    rows = pl.ds(pl.multiple_of(start, 128), 128)
    return jnp.concatenate([ref[:, rows, :].reshape(NZ * 128, 128) for ref in refs], axis=1)


def near_kernel(mine_ref, head_ref, *refs):
    swapped_refs, (out_ref, block_ref, semaphore) = refs[:3], refs[3:]
    fetch = pltpu.make_async_copy(head_ref.at[:, lax.axis_index("x")], block_ref, semaphore)
    fetch.start()
    start = lax.axis_index("c") * 128
    mine = gathered(mine_ref)
    fetch.wait()
    blocks = (block_ref,) + swapped_refs
    for pair in range(NX // 2):
        out_ref[pair] = jnp.dot(
            mine, head_block(blocks[2 * pair : 2 * pair + 2], start), preferred_element_type=F32
        )


def far_kernel(mine_ref, other_ref, near_ref, head_ref, *refs):
    swapped_refs, (out_ref, block_ref, semaphore) = refs[:3], refs[3:]
    x = lax.axis_index("x")
    fetch = pltpu.make_async_copy(head_ref.at[:, x], block_ref, semaphore)
    fetch.start()
    start = (1 - lax.axis_index("c")) * 128
    stat_row = lax.broadcasted_iota(jnp.int32, (16, 128), 0)
    stats = jnp.zeros((16, 128), F32)
    for y, (mine, other) in enumerate(zip(square_totals(mine_ref), square_totals(other_ref))):
        high, low = split_pair(jnp.sum(mine + other, axis=0, keepdims=True))
        stats = jnp.where(stat_row == y, high, jnp.where(stat_row == NY + y, low, stats))
    stats = stats.astype(BF16)
    other = gathered(other_ref)
    fetch.wait()
    blocks = (block_ref,) + swapped_refs
    for pair in range(NX // 2):
        partial = near_ref[pair] + jnp.dot(
            other, head_block(blocks[2 * pair : 2 * pair + 2], start), preferred_element_type=F32
        )
        partial = partial.astype(BF16)
        for k in range(2):
            target = lax.rem(x + NX - (2 * pair + k), NX)
            out_ref[target, 0:ROWS, :] = partial[:, 128 * k : 128 * k + 128]
            out_ref[target, ROWS : ROWS + 16, :] = stats


def logit_kernel(parts_ref, logits_ref, out_ref):
    stats = parts_ref[0, ROWS : ROWS + 16, :].astype(F32)
    for source in range(1, NX):
        stats += parts_ref[source, ROWS : ROWS + 16, :].astype(F32)
    factor = lax.rsqrt((stats[0:NY] + stats[NY:]) / D + 1e-05)
    tops, totals = [], []
    for block in range(4):
        rows = slice(128 * block, 128 * block + 128)
        logits = parts_ref[0, rows, :].astype(F32)
        for source in range(1, NX):
            logits += parts_ref[source, rows, :].astype(F32)
        column = jnp.concatenate(
            [to_column(factor[2 * block + k : 2 * block + k + 1])[0:64] for k in range(2)], axis=0
        )
        logits = logits * column
        logits_ref[rows, :] = logits
        top = jnp.max(logits, axis=1, keepdims=True)
        tops.append(to_row(top))
        totals.append(to_row(jnp.sum(jnp.exp(logits - top), axis=1, keepdims=True)))
    packed = jnp.concatenate(tops + totals, axis=0)
    for target in range(NY * NC):
        out_ref[target] = packed


def merge_stats(parts):
    tops = parts[:, 0:4, :]
    top = jnp.max(tops, axis=0)
    total = jnp.sum(jnp.exp(tops - top[None]) * parts[:, 4:8, :], axis=0)
    return top, total


def merge_kernel(parts_ref, out_ref):
    top, total = merge_stats(parts_ref[...])
    packed = jnp.concatenate([top, total], axis=0)
    for target in range(NZ * NX):
        out_ref[target] = packed


def vote_kernel(parts_ref, logits_ref, noise_ref, out_ref):
    top, total = merge_stats(parts_ref[...])
    averaged = jnp.zeros((QUERIES, 128), F32)
    for block in range(4):
        mass = jnp.exp(
            logits_ref[128 * block : 128 * block + 128, :] - to_column(top[block : block + 1])
        ) / to_column(total[block : block + 1])
        averaged += jnp.sum(mass.reshape(8, QUERIES, 128), axis=0)
    out_ref[...] = jnp.log(VOCAB * (averaged / PROMPTS)) + noise_ref[...]


def exchange(array, axes):
    return lax.all_to_all(array, axes, 0, 0, tiled=True)


def on_device(query, new_kv, cache, lengths, w_out, resid, norm_gain, head, noise):
    y, c = lax.axis_index("y"), lax.axis_index("c")
    x = lax.axis_index("x")
    blocks = head.reshape(NZ, NX, 256, 128)
    swapped = [
        lax.ppermute(
            lax.dynamic_index_in_dim(blocks, (x + k) % NX, 1, keepdims=False),
            "x",
            [(i, (i + k) % NX) for i in range(NX)],
        )
        for k in range(1, NX)
    ]
    resid_mine = jnp.swapaxes(
        lax.dynamic_slice(resid, (0, 4 * y, 128 * c), (QUERIES, 4, 128)), 0, 1
    ).reshape(64, 128)

    parts = call(
        attend_kernel,
        shape((NY * NC, 72, 128)),
        (lengths, query[:, 0, :], new_kv[:, :, 0, :], cache[:, 0]),
        "saaa",
        (
            pltpu.VMEM((QUERIES, D), BF16),
            pltpu.VMEM((2, QUERIES, KVH * HD), BF16),
            pltpu.VMEM((2, CACHE_ROWS, KVH * HD), BF16),
            pltpu.SemaphoreType.DMA((3,)),
        ),
        60,
    )
    parts = exchange(parts, ("c", "y"))
    attended = call(combine_kernel, shape((NZ * NX, 64, 128)), (parts,))
    attended = exchange(attended, ("x", "z"))
    partial = call(project_kernel, shape((NY * NC, 64, 128)), (attended, w_out))
    partial = exchange(partial, ("c", "y"))
    hidden = call(
        residual_kernel,
        shape((NZ * NY, 72, 128)),
        (partial, resid_mine, norm_gain.reshape(2, 128)),
    )
    mine = exchange(hidden, ("y", "z"))
    mine, *_ = lax.optimization_barrier((mine, *swapped))
    other = lax.ppermute(mine, "c", [(0, 1), (1, 0)])
    scratch = (pltpu.VMEM((NZ, 256, 128), BF16), pltpu.SemaphoreType.DMA)
    near = call(
        near_kernel,
        shape((NX // 2, ROWS, 256), F32),
        (mine, blocks, *swapped),
        "vavvv",
        scratch,
        12,
    )
    logits = call(
        far_kernel,
        shape((NX, ROWS + 16, 128)),
        (mine, other, near, blocks, *swapped),
        "vvvavvv",
        scratch,
        12,
    )
    logits = exchange(logits, ("x",))
    logits, stats = call(
        logit_kernel, (shape((ROWS, 128), F32), shape((NY * NC, 8, 128), F32)), (logits,)
    )
    stats = exchange(stats, ("c", "y"))
    stats = call(merge_kernel, shape((NZ * NX, 8, 128), F32), (stats,))
    stats = exchange(stats, ("x", "z"))
    return call(vote_kernel, shape((QUERIES, 128), F32), (stats, logits, noise))


def solution(mesh):
    torus = Mesh(mesh.devices.reshape(NZ, NX, NY, NC), MEMBER + TENSOR)
    placed = (
        P(None, MEMBER, None),
        P(None, None, MEMBER, None),
        P(None, MEMBER, TENSOR, None),
        P(MEMBER),
        P(TENSOR, MEMBER),
        P(None, None, MEMBER),
        P(MEMBER),
        P(None, MEMBER + TENSOR),
        P(None, MEMBER + TENSOR),
    )
    return jax.shard_map(
        on_device,
        mesh=torus,
        in_specs=placed,
        out_specs=P(None, MEMBER + TENSOR),
        check_vma=False,
    )
```

```python
import jax
import jax.numpy as jnp
from jax import lax
from jax.experimental import pallas as pl
from jax.experimental.pallas import tpu as pltpu
from jax.sharding import Mesh
from jax.sharding import PartitionSpec as P

NZ, NX, NY, NC = 8, 4, 8, 2
MEMBER = ("z", "x")
TENSOR = ("y", "c")

D = 8192
KVH = 8
GROUP = 8
HD = 128
QUERIES = 16
PROMPTS = 32
VOCAB = 65536
ROWS = PROMPTS * QUERIES
CACHE_ROWS = 64
LOW = -1e30

BF16 = jnp.bfloat16
F32 = jnp.float32


def call(body, out_shape, operands, spaces=None, scratch=(), mebibytes=8):
    vmem = pl.BlockSpec(memory_space=pltpu.VMEM)
    kinds = {
        "v": vmem,
        "s": pl.BlockSpec(memory_space=pltpu.SMEM),
        "a": pl.BlockSpec(memory_space=pltpu.HBM),
        "w": pl.BlockSpec(memory_space=pl.ANY),
    }
    return pl.pallas_call(
        body,
        out_shape=out_shape,
        in_specs=[kinds[s] for s in spaces or "v" * len(operands)],
        out_specs=jax.tree.map(lambda _: vmem, out_shape),
        scratch_shapes=scratch,
        compiler_params=pltpu.CompilerParams(vmem_limit_bytes=mebibytes * 2**20),
    )(*operands)


def shape(dims, dtype=BF16):
    return jax.ShapeDtypeStruct(dims, dtype)


def split_pair(value):
    high = value.astype(BF16).astype(F32)
    return high, value - high


def diagonal(rows):
    return lax.broadcasted_iota(jnp.int32, (rows, 128), 0) == lax.broadcasted_iota(
        jnp.int32, (rows, 128), 1
    )


def to_row(column):
    return jnp.sum(jnp.where(diagonal(column.shape[0]), column, 0.0), axis=0, keepdims=True)


def to_column(row):
    return jnp.sum(jnp.where(diagonal(128), row, 0.0), axis=1, keepdims=True)


def attend_kernel(length_ref, *refs):
    sources, out_ref, buffers, semaphores = refs[:3], refs[3], refs[4:7], refs[7]
    copies = [
        pltpu.make_async_copy(source, buffer, semaphores.at[i])
        for i, (source, buffer) in enumerate(zip(sources, buffers))
    ]
    for copy in copies:
        copy.start()
    query_ref, new_ref, cache_ref = buffers
    tensor_index = lax.axis_index("y") * NC + lax.axis_index("c")
    valid_rows = length_ref[0] - tensor_index * CACHE_ROWS
    positions = CACHE_ROWS + QUERIES
    row = lax.broadcasted_iota(jnp.int32, (positions, 128), 0)
    lane = lax.broadcasted_iota(jnp.int32, (positions, 128), 1)
    own_from = jnp.where(tensor_index == 0, CACHE_ROWS, positions)
    valid = ((row < CACHE_ROWS) & (row < valid_rows)) | (
        (row >= own_from) & (row - CACHE_ROWS == lane % QUERIES)
    )
    stat_row = lax.broadcasted_iota(jnp.int32, (8, 128), 0)
    for copy in copies:
        copy.wait()
    for g in range(KVH):
        columns = slice(g * HD, (g + 1) * HD)
        heads = [
            query_ref[:, (g * GROUP + r) * HD : (g * GROUP + r + 1) * HD] for r in range(GROUP)
        ]
        rows = jnp.concatenate(heads, axis=0)
        keys = jnp.concatenate([cache_ref[0, :, columns], new_ref[0, :, columns]], axis=0)
        values = jnp.concatenate([cache_ref[1, :, columns], new_ref[1, :, columns]], axis=0)
        scores = lax.dot_general(
            keys, rows, (((1,), (1,)), ((), ())), preferred_element_type=F32
        ) * HD ** (-0.5)
        scores = jnp.where(valid, scores, LOW)
        top = jnp.max(scores, axis=0, keepdims=True).astype(BF16).astype(F32)
        weights = jnp.where(valid, jnp.exp(scores - top), 0.0)
        high, low = split_pair(jnp.sum(weights, axis=0, keepdims=True))
        totals = lax.dot_general(
            weights.astype(BF16), values, (((0,), (0,)), ((), ())), preferred_element_type=F32
        ).astype(BF16)
        stats = jnp.where(
            stat_row == 0,
            top,
            jnp.where(stat_row == 1, high, jnp.where(stat_row == 2, low, 0.0)),
        ).astype(BF16)
        for half in range(2):
            out_ref[NY * half + g, 0:64, :] = totals[64 * half : 64 * half + 64]
            out_ref[NY * half + g, 64:72, :] = stats


def combine_kernel(parts_ref, _, out_ref):
    core = lax.axis_index("c")
    stats = parts_ref[:, 64:72, :].astype(F32)
    tops, totals = stats[:, 0, :], stats[:, 1, :] + stats[:, 2, :]
    weight = jnp.exp(tops - jnp.max(tops, axis=0, keepdims=True))
    scale = weight / jnp.sum(weight * totals, axis=0, keepdims=True)
    scale = jnp.concatenate([scale, jnp.zeros((112, 128), F32)], axis=0).T
    scale = jnp.where(core == 1, scale[64:, :], scale[:64, :])
    attended = jnp.zeros((64, 128), F32)
    for source in range(NY * NC):
        attended += scale[:, source : source + 1] * parts_ref[source, 0:64, :].astype(F32)
    attended = attended.astype(BF16)
    for target in range(NZ * NX):
        out_ref[target] = attended


def project_kernel(attended_ref, weight_ref, _, out_ref):
    features = jnp.concatenate(
        [attended_ref[:, 16 * r : 16 * r + 16, :].reshape(ROWS, HD) for r in range(4)], axis=1
    )
    partial = jnp.dot(features, weight_ref[...], preferred_element_type=F32).astype(BF16)
    for y in range(NY):
        rows = jnp.concatenate(
            [partial[16 * (NZ * x + y) : 16 * (NZ * x + y) + 16] for x in range(NX)], axis=0
        )
        for c in range(NC):
            out_ref[NY * c + y] = rows[:, 128 * c : 128 * c + 128]


def residual_kernel(parts_ref, resid_ref, _, __, out_ref):
    projected = parts_ref[0].astype(F32)
    for source in range(1, NY * NC):
        projected += parts_ref[source].astype(F32)
    hidden = (resid_ref[...].astype(F32) + projected).astype(BF16)
    for target in range(NZ * NY):
        out_ref[target] = hidden


def scaled_rows(ref, gains_ref, core):
    table = jnp.where(core == 1, gains_ref[:, 128:], gains_ref[:, :128])
    back = lax.rem(
        lax.axis_index("z") + NZ - lax.broadcasted_iota(jnp.int32, (NZ, 128), 0), NZ
    )
    gains = [jnp.sum(jnp.where(back == z, table, 0.0), axis=0, keepdims=True) for z in range(NZ)]
    rows, squares = [], []
    for y in range(NY):
        total = jnp.zeros((64, 128), F32)
        blocks = []
        for z in range(NZ):
            hidden = ref[NZ * y + z].astype(F32)
            total += hidden * hidden
            blocks.append((hidden * gains[z]).astype(BF16))
        rows.append(jnp.concatenate(blocks, axis=1))
        squares.append(to_row(jnp.sum(total, axis=1, keepdims=True)))
    return jnp.concatenate(rows, axis=0), jnp.concatenate(squares, axis=0)


def head_block(refs, start):
    rows = pl.ds(pl.multiple_of(start, 128), 128)
    return jnp.concatenate([ref[:, rows, :].reshape(NZ * 128, 128) for ref in refs], axis=1)


def near_kernel(mine_ref, gains_ref, head_ref, swapped_ref, out_ref, squares_ref, block_ref, semaphore):
    fetch = pltpu.make_async_copy(head_ref.at[:, lax.axis_index("x")], block_ref, semaphore)
    fetch.start()
    core = lax.axis_index("c")
    start = core * 128
    mine, squares_ref[...] = scaled_rows(mine_ref, gains_ref, core)
    fetch.wait()
    blocks = [block_ref] + [swapped_ref.at[k] for k in range(NX - 1)]
    for pair in range(NX // 2):
        out_ref[pair] = jnp.dot(
            mine, head_block(blocks[2 * pair : 2 * pair + 2], start), preferred_element_type=F32
        )


def far_kernel(
    other_ref, gains_ref, near_ref, squares_ref, head_ref, swapped_ref, out_ref, block_ref, semaphore
):
    x, core = lax.axis_index("x"), 1 - lax.axis_index("c")
    fetch = pltpu.make_async_copy(head_ref.at[:, x], block_ref, semaphore)
    fetch.start()
    start = core * 128
    other, squares = scaled_rows(other_ref, gains_ref, core)
    stats = jnp.concatenate(split_pair(squares + squares_ref[...]), axis=0).astype(BF16)
    fetch.wait()
    blocks = [block_ref] + [swapped_ref.at[k] for k in range(NX - 1)]
    for pair in range(NX // 2):
        partial = near_ref[pair] + jnp.dot(
            other, head_block(blocks[2 * pair : 2 * pair + 2], start), preferred_element_type=F32
        )
        partial = partial.astype(BF16)
        for k in range(2):
            target = lax.rem(x + NX - (2 * pair + k), NX)
            out_ref[target, 0:ROWS, :] = partial[:, 128 * k : 128 * k + 128]
            out_ref[target, ROWS : ROWS + 16, :] = stats


def logit_kernel(parts_ref, logits_ref, out_ref):
    stats = parts_ref[0, ROWS : ROWS + 16, :].astype(F32)
    for source in range(1, NX):
        stats += parts_ref[source, ROWS : ROWS + 16, :].astype(F32)
    factor = lax.rsqrt((stats[0:NY] + stats[NY:]) / D + 1e-05)
    tops, totals = [], []
    for block in range(4):
        rows = slice(128 * block, 128 * block + 128)
        logits = parts_ref[0, rows, :].astype(F32)
        for source in range(1, NX):
            logits += parts_ref[source, rows, :].astype(F32)
        column = jnp.concatenate(
            [to_column(factor[2 * block + k : 2 * block + k + 1])[0:64] for k in range(2)], axis=0
        )
        logits = logits * column
        logits_ref[rows, :] = logits
        top = jnp.max(logits, axis=1, keepdims=True)
        tops.append(to_row(top))
        totals.append(to_row(jnp.sum(jnp.exp(logits - top), axis=1, keepdims=True)))
    packed = jnp.concatenate(tops + totals, axis=0)
    for target in range(NY * NC):
        out_ref[target] = packed


def merge_stats(parts):
    tops = parts[:, 0:4, :]
    top = jnp.max(tops, axis=0)
    total = jnp.sum(jnp.exp(tops - top[None]) * parts[:, 4:8, :], axis=0)
    return top, total


def merge_kernel(parts_ref, out_ref):
    top, total = merge_stats(parts_ref[...])
    packed = jnp.concatenate([top, total], axis=0)
    for target in range(NZ * NX):
        out_ref[target] = packed


def vote_kernel(parts_ref, logits_ref, noise_ref, out_ref):
    top, total = merge_stats(parts_ref[...])
    averaged = jnp.zeros((QUERIES, 128), F32)
    for block in range(4):
        mass = jnp.exp(
            logits_ref[128 * block : 128 * block + 128, :] - to_column(top[block : block + 1])
        ) / to_column(total[block : block + 1])
        averaged += jnp.sum(mass.reshape(8, QUERIES, 128), axis=0)
    out_ref[...] = jnp.log(VOCAB * (averaged / PROMPTS)) + noise_ref[...]


def shift(array, axis, step):
    count = lax.axis_size(axis)
    return lax.ppermute(array, axis, [(i, (i + step) % count) for i in range(count)])


def exchange(array, axes):
    return lax.all_to_all(array, axes, 0, 0, tiled=True)


def on_device(query, new_kv, cache, lengths, w_out, resid, norm_gain, head, noise):
    y, c = lax.axis_index("y"), lax.axis_index("c")
    x = lax.axis_index("x")
    blocks = head.reshape(NZ, NX, 256, 128)
    swapped = [
        shift(lax.dynamic_index_in_dim(blocks, (x + k) % NX, 1, keepdims=False), "x", k)
        for k in range(1, NX)
    ]
    gains = [norm_gain.reshape(1, 256)]
    for step in (1, 2, 4):
        gains.append(jnp.concatenate([gains[-1], shift(gains[-1], "z", step)]))
    resid_mine = jnp.swapaxes(
        lax.dynamic_slice(resid, (0, 4 * y, 128 * c), (QUERIES, 4, 128)), 0, 1
    ).reshape(64, 128)

    parts = call(
        attend_kernel,
        shape((NY * NC, 72, 128)),
        (lengths, query[:, 0, :], new_kv[:, :, 0, :], cache[:, 0]),
        "saaa",
        (
            pltpu.VMEM((QUERIES, D), BF16),
            pltpu.VMEM((2, QUERIES, KVH * HD), BF16),
            pltpu.VMEM((2, CACHE_ROWS, KVH * HD), BF16),
            pltpu.SemaphoreType.DMA((3,)),
        ),
        60,
    )
    parts = exchange(parts, ("c", "y"))
    attended = call(combine_kernel, shape((NZ * NX, 64, 128)), (parts, gains[1]), "vw")
    attended = exchange(attended, ("x", "z"))
    partial = call(project_kernel, shape((NY * NC, 64, 128)), (attended, w_out, gains[2]), "vvw")
    partial = exchange(partial, ("c", "y"))
    hidden = call(
        residual_kernel,
        shape((NZ * NY, 64, 128)),
        (partial, resid_mine, swapped[1], gains[3]),
        "vvww",
    )
    mine = exchange(hidden, ("y", "z"))
    mine, swapped = lax.optimization_barrier((mine, jnp.stack(swapped)))
    other = shift(mine, "c", 1)
    scratch = (pltpu.VMEM((NZ, 256, 128), BF16), pltpu.SemaphoreType.DMA)
    near, squares = call(
        near_kernel,
        (shape((NX // 2, ROWS, 256), F32), shape((NY, 128), F32)),
        (mine, gains[3], blocks, swapped),
        "vvav",
        scratch,
        12,
    )
    logits = call(
        far_kernel,
        shape((NX, ROWS + 16, 128)),
        (other, gains[3], near, squares, blocks, swapped),
        "vvvvav",
        scratch,
        12,
    )
    logits = exchange(logits, ("x",))
    logits, stats = call(
        logit_kernel, (shape((ROWS, 128), F32), shape((NY * NC, 8, 128), F32)), (logits,)
    )
    stats = exchange(stats, ("c", "y"))
    stats = call(merge_kernel, shape((NZ * NX, 8, 128), F32), (stats,))
    stats = exchange(stats, ("x", "z"))
    return call(vote_kernel, shape((QUERIES, 128), F32), (stats, logits, noise))


def solution(mesh):
    torus = Mesh(mesh.devices.reshape(NZ, NX, NY, NC), MEMBER + TENSOR)
    placed = (
        P(None, MEMBER, None),
        P(None, None, MEMBER, None),
        P(None, MEMBER, TENSOR, None),
        P(MEMBER),
        P(TENSOR, MEMBER),
        P(None, None, MEMBER),
        P(MEMBER),
        P(None, MEMBER + TENSOR),
        P(None, MEMBER + TENSOR),
    )
    return jax.shard_map(
        on_device,
        mesh=torus,
        in_specs=placed,
        out_specs=P(None, MEMBER + TENSOR),
        check_vma=False,
    )
```

```python
import jax
import jax.numpy as jnp
from jax import lax
from jax.experimental import pallas as pl
from jax.experimental.pallas import tpu as pltpu
from jax.sharding import Mesh
from jax.sharding import PartitionSpec as P

NZ, NX, NY, NC = 8, 4, 8, 2
X = ("far", "near")
MEMBER = ("z",) + X
TENSOR = ("y", "c")

D = 8192
KVH = 8
GROUP = 8
HD = 128
QUERIES = 16
PROMPTS = 32
VOCAB = 65536
ROWS = PROMPTS * QUERIES
CACHE_ROWS = 64
LOW = -1e30

BF16 = jnp.bfloat16
F32 = jnp.float32


def call(body, out_shape, operands, spaces=None, scratch=(), mebibytes=8):
    vmem = pl.BlockSpec(memory_space=pltpu.VMEM)
    kinds = {
        "v": vmem,
        "s": pl.BlockSpec(memory_space=pltpu.SMEM),
        "a": pl.BlockSpec(memory_space=pltpu.HBM),
        "w": pl.BlockSpec(memory_space=pl.ANY),
    }
    return pl.pallas_call(
        body,
        out_shape=out_shape,
        in_specs=[kinds[s] for s in spaces or "v" * len(operands)],
        out_specs=jax.tree.map(lambda _: vmem, out_shape),
        scratch_shapes=scratch,
        compiler_params=pltpu.CompilerParams(vmem_limit_bytes=mebibytes * 2**20),
    )(*operands)


def x_index():
    return 2 * lax.axis_index("far") + lax.axis_index("near")


def shape(dims, dtype=BF16):
    return jax.ShapeDtypeStruct(dims, dtype)


def split_pair(value):
    high = value.astype(BF16).astype(F32)
    return high, value - high


def diagonal(rows):
    return lax.broadcasted_iota(jnp.int32, (rows, 128), 0) == lax.broadcasted_iota(
        jnp.int32, (rows, 128), 1
    )


def to_row(column):
    return jnp.sum(jnp.where(diagonal(column.shape[0]), column, 0.0), axis=0, keepdims=True)


def to_column(row):
    return jnp.sum(jnp.where(diagonal(128), row, 0.0), axis=1, keepdims=True)


def attend_kernel(length_ref, *refs):
    sources, out_ref, buffers, semaphores = refs[:3], refs[3], refs[4:7], refs[7]
    copies = [
        pltpu.make_async_copy(source, buffer, semaphores.at[i])
        for i, (source, buffer) in enumerate(zip(sources, buffers))
    ]
    for copy in copies:
        copy.start()
    query_ref, new_ref, cache_ref = buffers
    tensor_index = lax.axis_index("y") * NC + lax.axis_index("c")
    valid_rows = length_ref[0] - tensor_index * CACHE_ROWS
    positions = CACHE_ROWS + QUERIES
    row = lax.broadcasted_iota(jnp.int32, (positions, 128), 0)
    lane = lax.broadcasted_iota(jnp.int32, (positions, 128), 1)
    own_from = jnp.where(tensor_index == 0, CACHE_ROWS, positions)
    valid = ((row < CACHE_ROWS) & (row < valid_rows)) | (
        (row >= own_from) & (row - CACHE_ROWS == lane % QUERIES)
    )
    stat_row = lax.broadcasted_iota(jnp.int32, (16, 128), 0)
    for copy in copies:
        copy.wait()
    for g in range(KVH):
        columns = slice(g * HD, (g + 1) * HD)
        heads = [
            query_ref[:, (g * GROUP + r) * HD : (g * GROUP + r + 1) * HD] for r in range(GROUP)
        ]
        rows = jnp.concatenate(heads, axis=0)
        keys = jnp.concatenate([cache_ref[0, :, columns], new_ref[0, :, columns]], axis=0)
        values = jnp.concatenate([cache_ref[1, :, columns], new_ref[1, :, columns]], axis=0)
        scores = lax.dot_general(
            keys, rows, (((1,), (1,)), ((), ())), preferred_element_type=F32
        ) * HD ** (-0.5)
        scores = jnp.where(valid, scores, LOW)
        top = jnp.max(scores, axis=0, keepdims=True).astype(BF16).astype(F32)
        weights = jnp.where(valid, jnp.exp(scores - top), 0.0)
        high, low = split_pair(jnp.sum(weights, axis=0, keepdims=True))
        totals = lax.dot_general(
            weights.astype(BF16), values, (((0,), (0,)), ((), ())), preferred_element_type=F32
        ).astype(BF16)
        stats = jnp.where(
            stat_row == 0,
            top,
            jnp.where(stat_row == 1, high, jnp.where(stat_row == 2, low, 0.0)),
        ).astype(BF16)
        for half in range(2):
            out_ref[NY * half + g, 0:64, :] = totals[64 * half : 64 * half + 64]
            out_ref[NY * half + g, 64:80, :] = stats


def combine_kernel(parts_ref, _, __, out_ref):
    core = lax.axis_index("c")
    stats = parts_ref[:, 64:80, :].astype(F32)
    tops, totals = stats[:, 0, :], stats[:, 1, :] + stats[:, 2, :]
    weight = jnp.exp(tops - jnp.max(tops, axis=0, keepdims=True))
    scale = weight / jnp.sum(weight * totals, axis=0, keepdims=True)
    scale = jnp.concatenate([scale, jnp.zeros((112, 128), F32)], axis=0).T
    scale = jnp.where(core == 1, scale[64:, :], scale[:64, :])
    attended = jnp.zeros((64, 128), F32)
    for source in range(NY * NC):
        attended += scale[:, source : source + 1] * parts_ref[source, 0:64, :].astype(F32)
    attended = attended.astype(BF16)
    for target in range(2 * NZ):
        out_ref[target] = attended


def project_kernel(attended_ref, mine_ref, other_ref, out_ref):
    features = jnp.concatenate(
        [attended_ref[:, 16 * r : 16 * r + 16, :].reshape(ROWS // 2, HD) for r in range(4)], axis=1
    )
    near = lax.axis_index("near")
    for target, weight_ref in ((near, mine_ref), (1 - near, other_ref)):
        partial = jnp.dot(features, weight_ref[...], preferred_element_type=F32).astype(BF16)
        for y in range(NY):
            rows = jnp.concatenate(
                [partial[16 * (NZ * far + y) : 16 * (NZ * far + y) + 16] for far in range(2)],
                axis=0,
            )
            for c in range(NC):
                index = NC * NY * target + NY * c + y
                out_ref[index] = rows[:, 128 * c : 128 * c + 128]


def residual_kernel(parts_ref, resid_ref, _, __, out_ref):
    sums = []
    for near in range(2):
        total = parts_ref[NC * NY * near].astype(F32)
        for source in range(1, NC * NY):
            total += parts_ref[NC * NY * near + source].astype(F32)
        sums.append(total)
    projected = jnp.concatenate(
        [sums[x % 2][16 * (x // 2) : 16 * (x // 2) + 16] for x in range(NX)], axis=0
    )
    hidden = (resid_ref[...].astype(F32) + projected).astype(BF16)
    for target in range(NZ * NY):
        out_ref[target] = hidden


def scaled_rows(ref, gains_ref, core):
    table = jnp.where(core == 1, gains_ref[:, 128:], gains_ref[:, :128])
    back = lax.rem(
        lax.axis_index("z") + NZ - lax.broadcasted_iota(jnp.int32, (NZ, 128), 0), NZ
    )
    gains = [jnp.sum(jnp.where(back == z, table, 0.0), axis=0, keepdims=True) for z in range(NZ)]
    rows, squares = [], []
    for y in range(NY):
        total = jnp.zeros((64, 128), F32)
        blocks = []
        for z in range(NZ):
            hidden = ref[NZ * y + z].astype(F32)
            total += hidden * hidden
            blocks.append((hidden * gains[z]).astype(BF16))
        rows.append(jnp.concatenate(blocks, axis=1))
        squares.append(to_row(jnp.sum(total, axis=1, keepdims=True)))
    return jnp.concatenate(rows, axis=0), jnp.concatenate(squares, axis=0)


def head_block(refs, start):
    rows = pl.ds(pl.multiple_of(start, 128), 128)
    return jnp.concatenate([ref[:, rows, :].reshape(NZ * 128, 128) for ref in refs], axis=1)


def near_kernel(mine_ref, gains_ref, head_ref, swapped_ref, out_ref, squares_ref, block_ref, semaphore):
    fetch = pltpu.make_async_copy(head_ref.at[:, x_index()], block_ref, semaphore)
    fetch.start()
    core = lax.axis_index("c")
    start = core * 128
    mine, squares_ref[...] = scaled_rows(mine_ref, gains_ref, core)
    fetch.wait()
    blocks = [block_ref] + [swapped_ref.at[k] for k in range(NX - 1)]
    for pair in range(NX // 2):
        out_ref[pair] = jnp.dot(
            mine, head_block(blocks[2 * pair : 2 * pair + 2], start), preferred_element_type=F32
        )


def far_kernel(
    other_ref, gains_ref, near_ref, squares_ref, head_ref, swapped_ref, out_ref, block_ref, semaphore
):
    x, core = x_index(), 1 - lax.axis_index("c")
    fetch = pltpu.make_async_copy(head_ref.at[:, x], block_ref, semaphore)
    fetch.start()
    start = core * 128
    other, squares = scaled_rows(other_ref, gains_ref, core)
    stats = jnp.concatenate(split_pair(squares + squares_ref[...]), axis=0).astype(BF16)
    fetch.wait()
    blocks = [block_ref] + [swapped_ref.at[k] for k in range(NX - 1)]
    for pair in range(NX // 2):
        partial = near_ref[pair] + jnp.dot(
            other, head_block(blocks[2 * pair : 2 * pair + 2], start), preferred_element_type=F32
        )
        partial = partial.astype(BF16)
        for k in range(2):
            target = lax.rem(x + NX - (2 * pair + k), NX)
            out_ref[target, 0:ROWS, :] = partial[:, 128 * k : 128 * k + 128]
            out_ref[target, ROWS : ROWS + 16, :] = stats


def logit_kernel(parts_ref, logits_ref, out_ref):
    stats = parts_ref[0, ROWS : ROWS + 16, :].astype(F32)
    for source in range(1, NX):
        stats += parts_ref[source, ROWS : ROWS + 16, :].astype(F32)
    factor = lax.rsqrt((stats[0:NY] + stats[NY:]) / D + 1e-05)
    tops, totals = [], []
    for block in range(4):
        rows = slice(128 * block, 128 * block + 128)
        logits = parts_ref[0, rows, :].astype(F32)
        for source in range(1, NX):
            logits += parts_ref[source, rows, :].astype(F32)
        column = jnp.concatenate(
            [to_column(factor[2 * block + k : 2 * block + k + 1])[0:64] for k in range(2)], axis=0
        )
        logits = logits * column
        logits_ref[rows, :] = logits
        top = jnp.max(logits, axis=1, keepdims=True)
        tops.append(to_row(top))
        totals.append(to_row(jnp.sum(jnp.exp(logits - top), axis=1, keepdims=True)))
    packed = jnp.concatenate(tops + totals, axis=0)
    for target in range(NY * NC):
        out_ref[target] = packed


def merge_stats(parts):
    tops = parts[:, 0:4, :]
    top = jnp.max(tops, axis=0)
    total = jnp.sum(jnp.exp(tops - top[None]) * parts[:, 4:8, :], axis=0)
    return top, total


def merge_kernel(parts_ref, out_ref):
    top, total = merge_stats(parts_ref[...])
    packed = jnp.concatenate([top, total], axis=0)
    for target in range(NZ * NX):
        out_ref[target] = packed


def vote_kernel(parts_ref, logits_ref, noise_ref, out_ref):
    top, total = merge_stats(parts_ref[...])
    averaged = jnp.zeros((QUERIES, 128), F32)
    for block in range(4):
        mass = jnp.exp(
            logits_ref[128 * block : 128 * block + 128, :] - to_column(top[block : block + 1])
        ) / to_column(total[block : block + 1])
        averaged += jnp.sum(mass.reshape(8, QUERIES, 128), axis=0)
    out_ref[...] = jnp.log(VOCAB * (averaged / PROMPTS)) + noise_ref[...]


def shift(array, axis, step):
    count = lax.axis_size(axis)
    return lax.ppermute(array, axis, [(i, (i + step) % count) for i in range(count)])


def exchange(array, axes):
    return lax.all_to_all(array, axes, 0, 0, tiled=True)


def on_device(query, new_kv, cache, lengths, w_out, resid, norm_gain, head, noise):
    y, c = lax.axis_index("y"), lax.axis_index("c")
    x = x_index()
    blocks = head.reshape(NZ, NX, 256, 128)
    swapped = [
        shift(lax.dynamic_index_in_dim(blocks, (x + k) % NX, 1, keepdims=False), X, k)
        for k in range(1, NX)
    ]
    gains, arrived = norm_gain.reshape(1, 256), []
    for step in (1, 2, 4):
        arrived.append(shift(gains, "z", step))
        gains = jnp.concatenate([gains, arrived[-1]])
    resid_mine = jnp.swapaxes(
        lax.dynamic_slice(resid, (0, 4 * y, 128 * c), (QUERIES, 4, 128)), 0, 1
    ).reshape(64, 128)

    other_w = shift(w_out, "near", 1)
    parts = call(
        attend_kernel,
        shape((NY * NC, 80, 128)),
        (lengths, query[:, 0, :], new_kv[:, :, 0, :], cache[:, 0]),
        "saaa",
        (
            pltpu.VMEM((QUERIES, D), BF16),
            pltpu.VMEM((2, QUERIES, KVH * HD), BF16),
            pltpu.VMEM((2, CACHE_ROWS, KVH * HD), BF16),
            pltpu.SemaphoreType.DMA((3,)),
        ),
        60,
    )
    parts = exchange(parts, ("c", "y"))
    attended = call(combine_kernel, shape((2 * NZ, 64, 128)), (parts, arrived[0], other_w), "vww")
    attended = exchange(attended, ("far", "z"))
    partial = call(
        project_kernel,
        shape((2 * NC * NY, 32, 128)),
        (attended, w_out, other_w),
    )
    partial = exchange(partial, ("near", "c", "y"))
    hidden = call(
        residual_kernel,
        shape((NZ * NY, 64, 128)),
        (partial, resid_mine, swapped[1], arrived[1]),
        "vvww",
    )
    mine = exchange(hidden, ("y", "z"))
    mine, gains, swapped = lax.optimization_barrier((mine, gains, jnp.stack(swapped)))
    other = shift(mine, "c", 1)
    scratch = (pltpu.VMEM((NZ, 256, 128), BF16), pltpu.SemaphoreType.DMA)
    near, squares = call(
        near_kernel,
        (shape((NX // 2, ROWS, 256), F32), shape((NY, 128), F32)),
        (mine, gains, blocks, swapped),
        "vvav",
        scratch,
        12,
    )
    logits = call(
        far_kernel,
        shape((NX, ROWS + 16, 128)),
        (other, gains, near, squares, blocks, swapped),
        "vvvvav",
        scratch,
        12,
    )
    logits = exchange(logits, X)
    logits, stats = call(
        logit_kernel, (shape((ROWS, 128), F32), shape((NY * NC, 8, 128), F32)), (logits,)
    )
    stats = exchange(stats, ("c", "y"))
    stats = call(merge_kernel, shape((NZ * NX, 8, 128), F32), (stats,))
    stats = exchange(stats, X + ("z",))
    return call(vote_kernel, shape((QUERIES, 128), F32), (stats, logits, noise))


def solution(mesh):
    torus = Mesh(mesh.devices.reshape(NZ, 2, 2, NY, NC), MEMBER + TENSOR)
    placed = (
        P(None, MEMBER, None),
        P(None, None, MEMBER, None),
        P(None, MEMBER, TENSOR, None),
        P(MEMBER),
        P(TENSOR, MEMBER),
        P(None, None, MEMBER),
        P(MEMBER),
        P(None, MEMBER + TENSOR),
        P(None, MEMBER + TENSOR),
    )
    return jax.shard_map(
        on_device,
        mesh=torus,
        in_specs=placed,
        out_specs=P(None, MEMBER + TENSOR),
        check_vma=False,
    )
```

```python
import jax
import jax.numpy as jnp
from jax import lax
from jax.experimental import pallas as pl
from jax.experimental.pallas import tpu as pltpu
from jax.sharding import Mesh
from jax.sharding import PartitionSpec as P

NZ, NX, NY, NC = 8, 4, 8, 2
X = ("far", "near")
MEMBER = ("z",) + X
TENSOR = ("y", "c")

D = 8192
KVH = 8
GROUP = 8
HD = 128
QUERIES = 16
PROMPTS = 32
VOCAB = 65536
ROWS = PROMPTS * QUERIES
CACHE_ROWS = 64
LOW = -1e30

BF16 = jnp.bfloat16
F32 = jnp.float32


def call(body, out_shape, operands, spaces=None, scratch=(), mebibytes=8):
    vmem = pl.BlockSpec(memory_space=pltpu.VMEM)
    kinds = {
        "v": vmem,
        "s": pl.BlockSpec(memory_space=pltpu.SMEM),
        "a": pl.BlockSpec(memory_space=pltpu.HBM),
        "w": pl.BlockSpec(memory_space=pl.ANY),
    }
    return pl.pallas_call(
        body,
        out_shape=out_shape,
        in_specs=[kinds[s] for s in spaces or "v" * len(operands)],
        out_specs=jax.tree.map(lambda _: vmem, out_shape),
        scratch_shapes=scratch,
        compiler_params=pltpu.CompilerParams(vmem_limit_bytes=mebibytes * 2**20),
    )(*operands)


def x_index():
    return 2 * lax.axis_index("far") + lax.axis_index("near")


def shape(dims, dtype=BF16):
    return jax.ShapeDtypeStruct(dims, dtype)


def split_pair(value):
    high = value.astype(BF16).astype(F32)
    return high, value - high


def diagonal(rows):
    return lax.broadcasted_iota(jnp.int32, (rows, 128), 0) == lax.broadcasted_iota(
        jnp.int32, (rows, 128), 1
    )


def to_row(column):
    return jnp.sum(jnp.where(diagonal(column.shape[0]), column, 0.0), axis=0, keepdims=True)


def to_column(row):
    return jnp.sum(jnp.where(diagonal(128), row, 0.0), axis=1, keepdims=True)


def attend_kernel(length_ref, *refs):
    sources, out_ref, buffers, semaphores = refs[:3], refs[3], refs[4:7], refs[7]
    copies = [
        pltpu.make_async_copy(source, buffer, semaphores.at[i])
        for i, (source, buffer) in enumerate(zip(sources, buffers))
    ]
    for copy in copies:
        copy.start()
    query_ref, new_ref, cache_ref = buffers
    tensor_index = lax.axis_index("y") * NC + lax.axis_index("c")
    valid_rows = length_ref[0] - tensor_index * CACHE_ROWS
    positions = CACHE_ROWS + QUERIES
    row = lax.broadcasted_iota(jnp.int32, (positions, 128), 0)
    lane = lax.broadcasted_iota(jnp.int32, (positions, 128), 1)
    own_from = jnp.where(tensor_index == 0, CACHE_ROWS, positions)
    valid = ((row < CACHE_ROWS) & (row < valid_rows)) | (
        (row >= own_from) & (row - CACHE_ROWS == lane % QUERIES)
    )
    stat_row = lax.broadcasted_iota(jnp.int32, (16, 128), 0)
    for copy in copies:
        copy.wait()
    columns = [slice(g * HD, (g + 1) * HD) for g in range(KVH)]
    scores = []
    for g in range(KVH):
        heads = [
            query_ref[:, (g * GROUP + r) * HD : (g * GROUP + r + 1) * HD] for r in range(GROUP)
        ]
        keys = jnp.concatenate([cache_ref[0, :, columns[g]], new_ref[0, :, columns[g]]], axis=0)
        products = lax.dot_general(
            keys,
            jnp.concatenate(heads, axis=0),
            (((1,), (1,)), ((), ())),
            preferred_element_type=F32,
        )
        scores.append(jnp.where(valid, products * HD ** (-0.5), LOW))
    tops = [jnp.max(score, axis=0, keepdims=True).astype(BF16).astype(F32) for score in scores]
    weights = [
        jnp.where(valid, jnp.exp(score - top), 0.0) for score, top in zip(scores, tops)
    ]
    for g in range(KVH):
        values = jnp.concatenate([cache_ref[1, :, columns[g]], new_ref[1, :, columns[g]]], axis=0)
        high, low = split_pair(jnp.sum(weights[g], axis=0, keepdims=True))
        totals = lax.dot_general(
            weights[g].astype(BF16), values, (((0,), (0,)), ((), ())), preferred_element_type=F32
        ).astype(BF16)
        stats = jnp.where(
            stat_row == 0,
            tops[g],
            jnp.where(stat_row == 1, high, jnp.where(stat_row == 2, low, 0.0)),
        ).astype(BF16)
        for half in range(2):
            out_ref[NY * half + g, 0:64, :] = totals[64 * half : 64 * half + 64]
            out_ref[NY * half + g, 64:80, :] = stats


def combine_kernel(parts_ref, gain_ref, _, out_ref):
    core = lax.axis_index("c")
    stats = parts_ref[:, 64:80, :].astype(F32)
    tops, totals = stats[:, 0, :], stats[:, 1, :] + stats[:, 2, :]
    weight = jnp.exp(tops - jnp.max(tops, axis=0, keepdims=True))
    scale = weight / jnp.sum(weight * totals, axis=0, keepdims=True)
    scale = jnp.concatenate([scale, jnp.zeros((112, 128), F32)], axis=0).T
    scale = jnp.where(core == 1, scale[64:, :], scale[:64, :])
    attended = jnp.zeros((64, 128), F32)
    for source in range(NY * NC):
        attended += scale[:, source : source + 1] * parts_ref[source, 0:64, :].astype(F32)
    attended = attended.astype(BF16)
    stat_row = lax.broadcasted_iota(jnp.int32, (16, 128), 0)
    gains = jnp.zeros((16, 128), F32)
    for half in range(NC):
        high, low = split_pair(gain_ref[half : half + 1, :])
        gains = jnp.where(stat_row == half, high, jnp.where(stat_row == NC + half, low, gains))
    gains = gains.astype(BF16)
    for target in range(2 * NZ):
        out_ref[target, 0:64, :] = attended
        out_ref[target, 64:80, :] = gains


def project_kernel(attended_ref, mine_ref, other_ref, out_ref, gains_ref):
    features = jnp.concatenate(
        [attended_ref[:, 16 * r : 16 * r + 16, :].reshape(ROWS // 2, HD) for r in range(4)], axis=1
    )
    first = NZ * lax.axis_index("far")
    pairs = [attended_ref[first + z, 64:80, :].astype(F32) for z in range(NZ)]
    for half in range(NC):
        gains_ref[half] = jnp.concatenate(
            [pair[half : half + 1] + pair[NC + half : NC + half + 1] for pair in pairs], axis=0
        )
    near = lax.axis_index("near")
    for target, weight_ref in ((near, mine_ref), (1 - near, other_ref)):
        partial = jnp.dot(features, weight_ref[...], preferred_element_type=F32).astype(BF16)
        for y in range(NY):
            rows = jnp.concatenate(
                [partial[16 * (NZ * far + y) : 16 * (NZ * far + y) + 16] for far in range(2)],
                axis=0,
            )
            for c in range(NC):
                index = NC * NY * target + NY * c + y
                out_ref[index] = rows[:, 128 * c : 128 * c + 128]


def residual_kernel(parts_ref, resid_ref, _, out_ref):
    sums = []
    for near in range(2):
        total = parts_ref[NC * NY * near].astype(F32)
        for source in range(1, NC * NY):
            total += parts_ref[NC * NY * near + source].astype(F32)
        sums.append(total)
    projected = jnp.concatenate(
        [sums[x % 2][16 * (x // 2) : 16 * (x // 2) + 16] for x in range(NX)], axis=0
    )
    hidden = (resid_ref[...].astype(F32) + projected).astype(BF16)
    for target in range(NZ * NY):
        out_ref[target] = hidden


def scaled_rows(ref, gains_ref, core):
    table = jnp.where(core == 1, gains_ref[1], gains_ref[0])
    rows, squares = [], []
    for y in range(NY):
        total = jnp.zeros((64, 128), F32)
        blocks = []
        for z in range(NZ):
            hidden = ref[NZ * y + z].astype(F32)
            total += hidden * hidden
            blocks.append((hidden * table[z : z + 1]).astype(BF16))
        rows.append(jnp.concatenate(blocks, axis=1))
        squares.append(to_row(jnp.sum(total, axis=1, keepdims=True)))
    return jnp.concatenate(rows, axis=0), jnp.concatenate(squares, axis=0)


def head_block(refs, start):
    rows = pl.ds(pl.multiple_of(start, 128), 128)
    return jnp.concatenate([ref[:, rows, :].reshape(NZ * 128, 128) for ref in refs], axis=1)


def near_kernel(mine_ref, gains_ref, head_ref, swapped_ref, out_ref, squares_ref, block_ref, semaphore):
    fetch = pltpu.make_async_copy(head_ref.at[:, x_index()], block_ref, semaphore)
    fetch.start()
    core = lax.axis_index("c")
    start = core * 128
    mine, squares_ref[...] = scaled_rows(mine_ref, gains_ref, core)
    fetch.wait()
    blocks = [block_ref] + [swapped_ref.at[k] for k in range(NX - 1)]
    for pair in range(NX // 2):
        out_ref[pair] = jnp.dot(
            mine, head_block(blocks[2 * pair : 2 * pair + 2], start), preferred_element_type=F32
        )


def far_kernel(
    other_ref, gains_ref, near_ref, squares_ref, head_ref, swapped_ref, out_ref, block_ref, semaphore
):
    x, core = x_index(), 1 - lax.axis_index("c")
    fetch = pltpu.make_async_copy(head_ref.at[:, x], block_ref, semaphore)
    fetch.start()
    start = core * 128
    other, squares = scaled_rows(other_ref, gains_ref, core)
    stats = jnp.concatenate(split_pair(squares + squares_ref[...]), axis=0).astype(BF16)
    fetch.wait()
    blocks = [block_ref] + [swapped_ref.at[k] for k in range(NX - 1)]
    for pair in range(NX // 2):
        partial = near_ref[pair] + jnp.dot(
            other, head_block(blocks[2 * pair : 2 * pair + 2], start), preferred_element_type=F32
        )
        partial = partial.astype(BF16)
        for k in range(2):
            target = lax.rem(x + NX - (2 * pair + k), NX)
            out_ref[target, 0:ROWS, :] = partial[:, 128 * k : 128 * k + 128]
            out_ref[target, ROWS : ROWS + 16, :] = stats


def logit_kernel(parts_ref, logits_ref, out_ref):
    stats = parts_ref[0, ROWS : ROWS + 16, :].astype(F32)
    for source in range(1, NX):
        stats += parts_ref[source, ROWS : ROWS + 16, :].astype(F32)
    factor = lax.rsqrt((stats[0:NY] + stats[NY:]) / D + 1e-05)
    tops, totals = [], []
    for block in range(4):
        rows = slice(128 * block, 128 * block + 128)
        logits = parts_ref[0, rows, :].astype(F32)
        for source in range(1, NX):
            logits += parts_ref[source, rows, :].astype(F32)
        column = jnp.concatenate(
            [to_column(factor[2 * block + k : 2 * block + k + 1])[0:64] for k in range(2)], axis=0
        )
        logits = logits * column
        logits_ref[rows, :] = logits
        top = jnp.max(logits, axis=1, keepdims=True)
        tops.append(to_row(top))
        totals.append(to_row(jnp.sum(jnp.exp(logits - top), axis=1, keepdims=True)))
    packed = jnp.concatenate(tops + totals, axis=0)
    for target in range(NY * NC):
        out_ref[target] = packed


def merge_stats(parts):
    tops = parts[:, 0:4, :]
    top = jnp.max(tops, axis=0)
    total = jnp.sum(jnp.exp(tops - top[None]) * parts[:, 4:8, :], axis=0)
    return top, total


def merge_kernel(parts_ref, out_ref):
    top, total = merge_stats(parts_ref[...])
    packed = jnp.concatenate([top, total], axis=0)
    for target in range(NZ * NX):
        out_ref[target] = packed


def vote_kernel(parts_ref, logits_ref, noise_ref, out_ref):
    top, total = merge_stats(parts_ref[...])
    averaged = jnp.zeros((QUERIES, 128), F32)
    for block in range(4):
        mass = jnp.exp(
            logits_ref[128 * block : 128 * block + 128, :] - to_column(top[block : block + 1])
        ) / to_column(total[block : block + 1])
        averaged += jnp.sum(mass.reshape(8, QUERIES, 128), axis=0)
    out_ref[...] = jnp.log(VOCAB * (averaged / PROMPTS)) + noise_ref[...]


def shift(array, axis, step):
    count = lax.axis_size(axis)
    return lax.ppermute(array, axis, [(i, (i + step) % count) for i in range(count)])


def exchange(array, axes):
    return lax.all_to_all(array, axes, 0, 0, tiled=True)


def on_device(query, new_kv, cache, lengths, w_out, resid, norm_gain, head, noise):
    y, c = lax.axis_index("y"), lax.axis_index("c")
    x = x_index()
    blocks = head.reshape(NZ, NX, 256, 128)
    swapped = [
        shift(lax.dynamic_index_in_dim(blocks, (x + k) % NX, 1, keepdims=False), X, k)
        for k in range(1, NX)
    ]
    resid_mine = jnp.swapaxes(
        lax.dynamic_slice(resid, (0, 4 * y, 128 * c), (QUERIES, 4, 128)), 0, 1
    ).reshape(64, 128)

    other_w = shift(w_out, "near", 1)
    parts = call(
        attend_kernel,
        shape((NY * NC, 80, 128)),
        (lengths, query[:, 0, :], new_kv[:, :, 0, :], cache[:, 0]),
        "saaa",
        (
            pltpu.VMEM((QUERIES, D), BF16),
            pltpu.VMEM((2, QUERIES, KVH * HD), BF16),
            pltpu.VMEM((2, CACHE_ROWS, KVH * HD), BF16),
            pltpu.SemaphoreType.DMA((3,)),
        ),
        60,
    )
    parts = exchange(parts, ("c", "y"))
    attended = call(
        combine_kernel,
        shape((2 * NZ, 80, 128)),
        (parts, norm_gain.reshape(NC, 128), other_w),
        "vvw",
    )
    attended = exchange(attended, ("far", "z"))
    partial, gains = call(
        project_kernel,
        (shape((2 * NC * NY, 32, 128)), shape((NC, NZ, 128), F32)),
        (attended, w_out, other_w),
    )
    partial = exchange(partial, ("near", "c", "y"))
    hidden = call(
        residual_kernel,
        shape((NZ * NY, 64, 128)),
        (partial, resid_mine, swapped[1]),
        "vvw",
    )
    mine = exchange(hidden, ("y", "z"))
    mine, swapped = lax.optimization_barrier((mine, jnp.stack(swapped)))
    other = shift(mine, "c", 1)
    scratch = (pltpu.VMEM((NZ, 256, 128), BF16), pltpu.SemaphoreType.DMA)
    near, squares = call(
        near_kernel,
        (shape((NX // 2, ROWS, 256), F32), shape((NY, 128), F32)),
        (mine, gains, blocks, swapped),
        "vvav",
        scratch,
        12,
    )
    logits = call(
        far_kernel,
        shape((NX, ROWS + 16, 128)),
        (other, gains, near, squares, blocks, swapped),
        "vvvvav",
        scratch,
        12,
    )
    logits = exchange(logits, X)
    logits, stats = call(
        logit_kernel, (shape((ROWS, 128), F32), shape((NY * NC, 8, 128), F32)), (logits,)
    )
    stats = exchange(stats, ("c", "y"))
    stats = call(merge_kernel, shape((NZ * NX, 8, 128), F32), (stats,))
    stats = exchange(stats, X + ("z",))
    return call(vote_kernel, shape((QUERIES, 128), F32), (stats, logits, noise))


def solution(mesh):
    torus = Mesh(mesh.devices.reshape(NZ, 2, 2, NY, NC), MEMBER + TENSOR)
    placed = (
        P(None, MEMBER, None),
        P(None, None, MEMBER, None),
        P(None, MEMBER, TENSOR, None),
        P(MEMBER),
        P(TENSOR, MEMBER),
        P(None, None, MEMBER),
        P(MEMBER),
        P(None, MEMBER + TENSOR),
        P(None, MEMBER + TENSOR),
    )
    return jax.shard_map(
        on_device,
        mesh=torus,
        in_specs=placed,
        out_specs=P(None, MEMBER + TENSOR),
        check_vma=False,
    )
```

```python
import jax
import jax.numpy as jnp
from jax import lax
from jax.experimental import pallas as pl
from jax.experimental.pallas import tpu as pltpu
from jax.sharding import Mesh
from jax.sharding import PartitionSpec as P

NZ, NX, NY, NC = 8, 4, 8, 2
X = ("far", "near")
MEMBER = ("z",) + X
TENSOR = ("y", "c")

D = 8192
KVH = 8
GROUP = 8
HD = 128
QUERIES = 16
PROMPTS = 32
VOCAB = 65536
ROWS = PROMPTS * QUERIES
CACHE_ROWS = 64
LOW = -1e30

BF16 = jnp.bfloat16
F32 = jnp.float32


def call(body, out_shape, operands, spaces=None, scratch=(), mebibytes=8):
    vmem = pl.BlockSpec(memory_space=pltpu.VMEM)
    kinds = {
        "v": vmem,
        "s": pl.BlockSpec(memory_space=pltpu.SMEM),
        "a": pl.BlockSpec(memory_space=pltpu.HBM),
        "w": pl.BlockSpec(memory_space=pl.ANY),
    }
    return pl.pallas_call(
        body,
        out_shape=out_shape,
        in_specs=[kinds[s] for s in spaces or "v" * len(operands)],
        out_specs=jax.tree.map(lambda _: vmem, out_shape),
        scratch_shapes=scratch,
        compiler_params=pltpu.CompilerParams(vmem_limit_bytes=mebibytes * 2**20),
    )(*operands)


def x_index():
    return 2 * lax.axis_index("far") + lax.axis_index("near")


def shape(dims, dtype=BF16):
    return jax.ShapeDtypeStruct(dims, dtype)


def split_pair(value):
    high = value.astype(BF16).astype(F32)
    return high, value - high


def diagonal(rows):
    return lax.broadcasted_iota(jnp.int32, (rows, 128), 0) == lax.broadcasted_iota(
        jnp.int32, (rows, 128), 1
    )


def to_row(column):
    return jnp.sum(jnp.where(diagonal(column.shape[0]), column, 0.0), axis=0, keepdims=True)


def to_column(row):
    return jnp.sum(jnp.where(diagonal(128), row, 0.0), axis=1, keepdims=True)


def attend_kernel(length_ref, *refs):
    sources, out_ref, buffers, semaphores = refs[:3], refs[3], refs[4:7], refs[7]
    copies = [
        pltpu.make_async_copy(source, buffer, semaphores.at[i])
        for i, (source, buffer) in enumerate(zip(sources, buffers))
    ]
    for copy in copies:
        copy.start()
    query_ref, new_ref, cache_ref = buffers
    tensor_index = lax.axis_index("y") * NC + lax.axis_index("c")
    valid_rows = length_ref[0] - tensor_index * CACHE_ROWS
    positions = CACHE_ROWS + QUERIES
    row = lax.broadcasted_iota(jnp.int32, (positions, 128), 0)
    lane = lax.broadcasted_iota(jnp.int32, (positions, 128), 1)
    own_from = jnp.where(tensor_index == 0, CACHE_ROWS, positions)
    valid = ((row < CACHE_ROWS) & (row < valid_rows)) | (
        (row >= own_from) & (row - CACHE_ROWS == lane % QUERIES)
    )
    stat_row = lax.broadcasted_iota(jnp.int32, (16, 128), 0)
    for copy in copies:
        copy.wait()
    columns = [slice(g * HD, (g + 1) * HD) for g in range(KVH)]
    scores = []
    for g in range(KVH):
        heads = [
            query_ref[:, (g * GROUP + r) * HD : (g * GROUP + r + 1) * HD] for r in range(GROUP)
        ]
        keys = jnp.concatenate([cache_ref[0, :, columns[g]], new_ref[0, :, columns[g]]], axis=0)
        products = lax.dot_general(
            keys,
            jnp.concatenate(heads, axis=0),
            (((1,), (1,)), ((), ())),
            preferred_element_type=F32,
        )
        scores.append(jnp.where(valid, products * HD ** (-0.5), LOW))
    tops = [jnp.max(score, axis=0, keepdims=True).astype(BF16).astype(F32) for score in scores]
    weights = [
        jnp.where(valid, jnp.exp(score - top), 0.0) for score, top in zip(scores, tops)
    ]
    for g in range(KVH):
        values = jnp.concatenate([cache_ref[1, :, columns[g]], new_ref[1, :, columns[g]]], axis=0)
        high, low = split_pair(jnp.sum(weights[g], axis=0, keepdims=True))
        totals = lax.dot_general(
            weights[g].astype(BF16), values, (((0,), (0,)), ((), ())), preferred_element_type=F32
        ).astype(BF16)
        stats = jnp.where(
            stat_row == 0,
            tops[g],
            jnp.where(stat_row == 1, high, jnp.where(stat_row == 2, low, 0.0)),
        ).astype(BF16)
        for half in range(2):
            out_ref[NY * half + g, 0:64, :] = totals[64 * half : 64 * half + 64]
            out_ref[NY * half + g, 64:80, :] = stats


def combine_kernel(parts_ref, gain_ref, _, out_ref):
    core = lax.axis_index("c")
    stats = parts_ref[:, 64:80, :].astype(F32)
    tops, totals = stats[:, 0, :], stats[:, 1, :] + stats[:, 2, :]
    weight = jnp.exp(tops - jnp.max(tops, axis=0, keepdims=True))
    scale = weight / jnp.sum(weight * totals, axis=0, keepdims=True)
    scale = jnp.concatenate([scale, jnp.zeros((112, 128), F32)], axis=0).T
    scale = jnp.where(core == 1, scale[64:, :], scale[:64, :])
    attended = jnp.zeros((64, 128), F32)
    for source in range(NY * NC):
        attended += scale[:, source : source + 1] * parts_ref[source, 0:64, :].astype(F32)
    attended = attended.astype(BF16)
    stat_row = lax.broadcasted_iota(jnp.int32, (16, 128), 0)
    gains = jnp.zeros((16, 128), F32)
    for half in range(NC):
        high, low = split_pair(gain_ref[half : half + 1, :])
        gains = jnp.where(stat_row == half, high, jnp.where(stat_row == NC + half, low, gains))
    gains = gains.astype(BF16)
    for target in range(2 * NZ):
        out_ref[target, 0:64, :] = attended
        out_ref[target, 64:80, :] = gains


def project_kernel(attended_ref, mine_ref, other_ref, out_ref, gains_ref):
    features = jnp.concatenate(
        [attended_ref[:, 16 * r : 16 * r + 16, :].reshape(ROWS // 2, HD) for r in range(4)], axis=1
    )
    first = NZ * lax.axis_index("far")
    pairs = [attended_ref[first + z, 64:80, :].astype(F32) for z in range(NZ)]
    for half in range(NC):
        gains_ref[half] = jnp.concatenate(
            [pair[half : half + 1] + pair[NC + half : NC + half + 1] for pair in pairs], axis=0
        )
    near = lax.axis_index("near")
    for target, weight_ref in ((near, mine_ref), (1 - near, other_ref)):
        partial = jnp.dot(features, weight_ref[...], preferred_element_type=F32).astype(BF16)
        for y in range(NY):
            rows = jnp.concatenate(
                [partial[16 * (NZ * far + y) : 16 * (NZ * far + y) + 16] for far in range(2)],
                axis=0,
            )
            for c in range(NC):
                index = NC * NY * target + NY * c + y
                out_ref[index] = rows[:, 128 * c : 128 * c + 128]


def residual_kernel(parts_ref, resid_ref, _, out_ref):
    sums = []
    for near in range(2):
        total = parts_ref[NC * NY * near].astype(F32)
        for source in range(1, NC * NY):
            total += parts_ref[NC * NY * near + source].astype(F32)
        sums.append(total)
    projected = jnp.concatenate(
        [sums[x % 2][16 * (x // 2) : 16 * (x // 2) + 16] for x in range(NX)], axis=0
    )
    hidden = (resid_ref[...].astype(F32) + projected).astype(BF16)
    for target in range(NZ * NY):
        out_ref[target] = hidden


def scaled_rows(ref, gains_ref, core):
    table = jnp.where(core == 1, gains_ref[1], gains_ref[0])
    rows, squares = [], []
    for y in range(NY):
        total = jnp.zeros((64, 128), F32)
        blocks = []
        for z in range(NZ):
            hidden = ref[NZ * y + z].astype(F32)
            total += hidden * hidden
            blocks.append((hidden * table[z : z + 1]).astype(BF16))
        rows.append(jnp.concatenate(blocks, axis=1))
        squares.append(to_row(jnp.sum(total, axis=1, keepdims=True)))
    return jnp.concatenate(rows, axis=0), jnp.concatenate(squares, axis=0)


def head_block(refs, start):
    rows = pl.ds(pl.multiple_of(start, 128), 128)
    return jnp.concatenate([ref[:, rows, :].reshape(NZ * 128, 128) for ref in refs], axis=1)


def near_kernel(mine_ref, gains_ref, head_ref, swapped_ref, out_ref, squares_ref, block_ref, semaphore):
    fetch = pltpu.make_async_copy(head_ref.at[:, x_index()], block_ref, semaphore)
    fetch.start()
    core = lax.axis_index("c")
    start = core * 128
    mine, squares_ref[...] = scaled_rows(mine_ref, gains_ref, core)
    fetch.wait()
    blocks = [block_ref] + [swapped_ref.at[k] for k in range(NX - 1)]
    for pair in range(NX // 2):
        out_ref[pair] = jnp.dot(
            mine, head_block(blocks[2 * pair : 2 * pair + 2], start), preferred_element_type=F32
        )


def far_kernel(
    other_ref, gains_ref, near_ref, squares_ref, head_ref, swapped_ref, out_ref, block_ref, semaphore
):
    x, core = x_index(), 1 - lax.axis_index("c")
    fetch = pltpu.make_async_copy(head_ref.at[:, x], block_ref, semaphore)
    fetch.start()
    start = core * 128
    other, squares = scaled_rows(other_ref, gains_ref, core)
    stats = jnp.concatenate(split_pair(squares + squares_ref[...]), axis=0).astype(BF16)
    fetch.wait()
    blocks = [block_ref] + [swapped_ref.at[k] for k in range(NX - 1)]
    for pair in range(NX // 2):
        partial = near_ref[pair] + jnp.dot(
            other, head_block(blocks[2 * pair : 2 * pair + 2], start), preferred_element_type=F32
        )
        partial = partial.astype(BF16)
        for k in range(2):
            target = lax.rem(x + NX - (2 * pair + k), NX)
            out_ref[target, 0:ROWS, :] = partial[:, 128 * k : 128 * k + 128]
            out_ref[target, ROWS : ROWS + 16, :] = stats


def logit_kernel(parts_ref, logits_ref, out_ref):
    stats = parts_ref[0, ROWS : ROWS + 16, :].astype(F32)
    for source in range(1, NX):
        stats += parts_ref[source, ROWS : ROWS + 16, :].astype(F32)
    factor = lax.rsqrt((stats[0:NY] + stats[NY:]) / D + 1e-05)
    masses = []
    for block in range(4):
        rows = slice(128 * block, 128 * block + 128)
        logits = parts_ref[0, rows, :].astype(F32)
        for source in range(1, NX):
            logits += parts_ref[source, rows, :].astype(F32)
        column = jnp.concatenate(
            [to_column(factor[2 * block + k : 2 * block + k + 1])[0:64] for k in range(2)], axis=0
        )
        logits = logits * column
        logits_ref[rows, :] = logits
        top = jnp.max(logits, axis=1, keepdims=True)
        total = jnp.sum(jnp.exp(logits - top), axis=1, keepdims=True)
        masses.append(to_row(top + jnp.log(total)))
    packed = jnp.concatenate(masses, axis=0)
    for target in range(NY * NC):
        out_ref[target] = packed


def merge_masses(masses):
    top = jnp.max(masses, axis=0)
    return top + jnp.log(jnp.sum(jnp.exp(masses - top[None]), axis=0))


def merge_kernel(parts_ref, out_ref):
    merged = merge_masses(parts_ref[...])
    for target in range(NZ * NX):
        out_ref[target] = merged


def vote_kernel(parts_ref, logits_ref, noise_ref, out_ref):
    merged = merge_masses(parts_ref[...])
    averaged = jnp.zeros((QUERIES, 128), F32)
    for block in range(4):
        mass = jnp.exp(
            logits_ref[128 * block : 128 * block + 128, :] - to_column(merged[block : block + 1])
        )
        averaged += jnp.sum(mass.reshape(8, QUERIES, 128), axis=0)
    out_ref[...] = jnp.log(VOCAB * (averaged / PROMPTS)) + noise_ref[...]


def shift(array, axis, step):
    count = lax.axis_size(axis)
    return lax.ppermute(array, axis, [(i, (i + step) % count) for i in range(count)])


def exchange(array, axes):
    return lax.all_to_all(array, axes, 0, 0, tiled=True)


def on_device(query, new_kv, cache, lengths, w_out, resid, norm_gain, head, noise):
    y, c = lax.axis_index("y"), lax.axis_index("c")
    x = x_index()
    blocks = head.reshape(NZ, NX, 256, 128)
    swapped = [
        shift(lax.dynamic_index_in_dim(blocks, (x + k) % NX, 1, keepdims=False), X, k)
        for k in range(1, NX)
    ]
    resid_mine = jnp.swapaxes(
        lax.dynamic_slice(resid, (0, 4 * y, 128 * c), (QUERIES, 4, 128)), 0, 1
    ).reshape(64, 128)

    other_w = shift(w_out, "near", 1)
    parts = call(
        attend_kernel,
        shape((NY * NC, 80, 128)),
        (lengths, query[:, 0, :], new_kv[:, :, 0, :], cache[:, 0]),
        "saaa",
        (
            pltpu.VMEM((QUERIES, D), BF16),
            pltpu.VMEM((2, QUERIES, KVH * HD), BF16),
            pltpu.VMEM((2, CACHE_ROWS, KVH * HD), BF16),
            pltpu.SemaphoreType.DMA((3,)),
        ),
        60,
    )
    parts = exchange(parts, ("c", "y"))
    attended = call(
        combine_kernel,
        shape((2 * NZ, 80, 128)),
        (parts, norm_gain.reshape(NC, 128), other_w),
        "vvw",
    )
    attended = exchange(attended, ("far", "z"))
    partial, gains = call(
        project_kernel,
        (shape((2 * NC * NY, 32, 128)), shape((NC, NZ, 128), F32)),
        (attended, w_out, other_w),
    )
    partial = exchange(partial, ("near", "c", "y"))
    hidden = call(
        residual_kernel,
        shape((NZ * NY, 64, 128)),
        (partial, resid_mine, swapped[1]),
        "vvw",
    )
    mine = exchange(hidden, ("y", "z"))
    mine, swapped = lax.optimization_barrier((mine, jnp.stack(swapped)))
    other = shift(mine, "c", 1)
    scratch = (pltpu.VMEM((NZ, 256, 128), BF16), pltpu.SemaphoreType.DMA)
    near, squares = call(
        near_kernel,
        (shape((NX // 2, ROWS, 256), F32), shape((NY, 128), F32)),
        (mine, gains, blocks, swapped),
        "vvav",
        scratch,
        12,
    )
    logits = call(
        far_kernel,
        shape((NX, ROWS + 16, 128)),
        (other, gains, near, squares, blocks, swapped),
        "vvvvav",
        scratch,
        12,
    )
    logits = exchange(logits, X)
    logits, stats = call(
        logit_kernel, (shape((ROWS, 128), F32), shape((NY * NC, 4, 128), F32)), (logits,)
    )
    stats = exchange(stats, ("c", "y"))
    stats = call(merge_kernel, shape((NZ * NX, 4, 128), F32), (stats,))
    stats = exchange(stats, X + ("z",))
    return call(vote_kernel, shape((QUERIES, 128), F32), (stats, logits, noise))


def solution(mesh):
    torus = Mesh(mesh.devices.reshape(NZ, 2, 2, NY, NC), MEMBER + TENSOR)
    placed = (
        P(None, MEMBER, None),
        P(None, None, MEMBER, None),
        P(None, MEMBER, TENSOR, None),
        P(MEMBER),
        P(TENSOR, MEMBER),
        P(None, None, MEMBER),
        P(MEMBER),
        P(None, MEMBER + TENSOR),
        P(None, MEMBER + TENSOR),
    )
    return jax.shard_map(
        on_device,
        mesh=torus,
        in_specs=placed,
        out_specs=P(None, MEMBER + TENSOR),
        check_vma=False,
    )
```

```python
import jax
import jax.numpy as jnp
from jax import lax
from jax.experimental import pallas as pl
from jax.experimental.pallas import tpu as pltpu
from jax.sharding import Mesh
from jax.sharding import PartitionSpec as P

NZ, NX, NY, NC = 8, 4, 8, 2
X = ("far", "near")
MEMBER = ("z",) + X
TENSOR = ("y", "c")

D = 8192
KVH = 8
GROUP = 8
HD = 128
QUERIES = 16
PROMPTS = 32
VOCAB = 65536
ROWS = PROMPTS * QUERIES
CACHE_ROWS = 64
LOW = -1e30

BF16 = jnp.bfloat16
F32 = jnp.float32


def call(body, out_shape, operands, spaces=None, scratch=(), mebibytes=8):
    vmem = pl.BlockSpec(memory_space=pltpu.VMEM)
    kinds = {
        "v": vmem,
        "s": pl.BlockSpec(memory_space=pltpu.SMEM),
        "a": pl.BlockSpec(memory_space=pltpu.HBM),
        "w": pl.BlockSpec(memory_space=pl.ANY),
    }
    return pl.pallas_call(
        body,
        out_shape=out_shape,
        in_specs=[kinds[s] for s in spaces or "v" * len(operands)],
        out_specs=jax.tree.map(lambda _: vmem, out_shape),
        scratch_shapes=scratch,
        compiler_params=pltpu.CompilerParams(vmem_limit_bytes=mebibytes * 2**20),
    )(*operands)


def x_index():
    return 2 * lax.axis_index("far") + lax.axis_index("near")


def shape(dims, dtype=BF16):
    return jax.ShapeDtypeStruct(dims, dtype)


def split_pair(value):
    high = value.astype(BF16).astype(F32)
    return high, value - high


def diagonal(rows):
    return lax.broadcasted_iota(jnp.int32, (rows, 128), 0) == lax.broadcasted_iota(
        jnp.int32, (rows, 128), 1
    )


def to_row(column):
    return jnp.sum(jnp.where(diagonal(column.shape[0]), column, 0.0), axis=0, keepdims=True)


def to_column(row):
    return jnp.sum(jnp.where(diagonal(128), row, 0.0), axis=1, keepdims=True)


def attend_kernel(length_ref, *refs):
    sources, out_ref, buffers, semaphores = refs[:3], refs[3], refs[4:7], refs[7]
    copies = [
        pltpu.make_async_copy(source, buffer, semaphores.at[i])
        for i, (source, buffer) in enumerate(zip(sources, buffers))
    ]
    for copy in copies:
        copy.start()
    query_ref, new_ref, cache_ref = buffers
    tensor_index = lax.axis_index("y") * NC + lax.axis_index("c")
    valid_rows = length_ref[0] - tensor_index * CACHE_ROWS
    positions = CACHE_ROWS + QUERIES
    row = lax.broadcasted_iota(jnp.int32, (positions, 128), 0)
    lane = lax.broadcasted_iota(jnp.int32, (positions, 128), 1)
    own_from = jnp.where(tensor_index == 0, CACHE_ROWS, positions)
    valid = ((row < CACHE_ROWS) & (row < valid_rows)) | (
        (row >= own_from) & (row - CACHE_ROWS == lane % QUERIES)
    )
    stat_row = lax.broadcasted_iota(jnp.int32, (16, 128), 0)
    for copy in copies:
        copy.wait()
    columns = [slice(g * HD, (g + 1) * HD) for g in range(KVH)]
    scores = []
    for g in range(KVH):
        heads = [
            query_ref[:, (g * GROUP + r) * HD : (g * GROUP + r + 1) * HD] for r in range(GROUP)
        ]
        keys = jnp.concatenate([cache_ref[0, :, columns[g]], new_ref[0, :, columns[g]]], axis=0)
        products = lax.dot_general(
            keys,
            jnp.concatenate(heads, axis=0),
            (((1,), (1,)), ((), ())),
            preferred_element_type=F32,
        )
        scores.append(jnp.where(valid, products * HD ** (-0.5), LOW))
    tops = [jnp.max(score, axis=0, keepdims=True).astype(BF16).astype(F32) for score in scores]
    weights = [
        jnp.where(valid, jnp.exp(score - top), 0.0) for score, top in zip(scores, tops)
    ]
    for g in range(KVH):
        values = jnp.concatenate([cache_ref[1, :, columns[g]], new_ref[1, :, columns[g]]], axis=0)
        high, low = split_pair(jnp.sum(weights[g], axis=0, keepdims=True))
        totals = lax.dot_general(
            weights[g].astype(BF16), values, (((0,), (0,)), ((), ())), preferred_element_type=F32
        ).astype(BF16)
        stats = jnp.where(
            stat_row == 0,
            tops[g],
            jnp.where(stat_row == 1, high, jnp.where(stat_row == 2, low, 0.0)),
        ).astype(BF16)
        for half in range(2):
            out_ref[NY * half + g, 0:64, :] = totals[64 * half : 64 * half + 64]
            out_ref[NY * half + g, 64:80, :] = stats


def combine_kernel(parts_ref, gain_ref, _, out_ref):
    core = lax.axis_index("c")
    stats = parts_ref[:, 64:80, :].astype(F32)
    tops, totals = stats[:, 0, :], stats[:, 1, :] + stats[:, 2, :]
    weight = jnp.exp(tops - jnp.max(tops, axis=0, keepdims=True))
    scale = weight / jnp.sum(weight * totals, axis=0, keepdims=True)
    scale = jnp.concatenate([scale, jnp.zeros((112, 128), F32)], axis=0).T
    scale = jnp.where(core == 1, scale[64:, :], scale[:64, :])
    attended = jnp.zeros((64, 128), F32)
    for source in range(NY * NC):
        attended += scale[:, source : source + 1] * parts_ref[source, 0:64, :].astype(F32)
    attended = attended.astype(BF16)
    stat_row = lax.broadcasted_iota(jnp.int32, (16, 128), 0)
    gains = jnp.zeros((16, 128), F32)
    for half in range(NC):
        high, low = split_pair(gain_ref[half : half + 1, :])
        gains = jnp.where(stat_row == half, high, jnp.where(stat_row == NC + half, low, gains))
    gains = gains.astype(BF16)
    for target in range(2 * NZ):
        out_ref[target, 0:64, :] = attended
        out_ref[target, 64:80, :] = gains


def project_kernel(attended_ref, mine_ref, other_ref, out_ref, gains_ref):
    features = jnp.concatenate(
        [attended_ref[:, 16 * r : 16 * r + 16, :].reshape(ROWS // 2, HD) for r in range(4)], axis=1
    )
    first = NZ * lax.axis_index("far")
    pairs = [attended_ref[first + z, 64:80, :].astype(F32) for z in range(NZ)]
    for half in range(NC):
        gains_ref[half] = jnp.concatenate(
            [pair[half : half + 1] + pair[NC + half : NC + half + 1] for pair in pairs], axis=0
        )
    near = lax.axis_index("near")
    for target, weight_ref in ((near, mine_ref), (1 - near, other_ref)):
        partial = jnp.dot(features, weight_ref[...], preferred_element_type=F32).astype(BF16)
        for y in range(NY):
            rows = jnp.concatenate(
                [partial[16 * (NZ * far + y) : 16 * (NZ * far + y) + 16] for far in range(2)],
                axis=0,
            )
            for c in range(NC):
                index = NC * NY * target + NY * c + y
                out_ref[index] = rows[:, 128 * c : 128 * c + 128]


def residual_kernel(parts_ref, resid_ref, _, out_ref):
    sums = []
    for near in range(2):
        total = parts_ref[NC * NY * near].astype(F32)
        for source in range(1, NC * NY):
            total += parts_ref[NC * NY * near + source].astype(F32)
        sums.append(total)
    projected = jnp.concatenate(
        [sums[x % 2][16 * (x // 2) : 16 * (x // 2) + 16] for x in range(NX)], axis=0
    )
    hidden = (resid_ref[...].astype(F32) + projected).astype(BF16)
    for target in range(NZ * NY):
        out_ref[target] = hidden


def scaled_rows(ref, gains_ref, core):
    table = jnp.where(core == 1, gains_ref[1], gains_ref[0])
    rows, squares = [], []
    for y in range(NY):
        total = jnp.zeros((64, 128), F32)
        blocks = []
        for z in range(NZ):
            hidden = ref[NZ * y + z].astype(F32)
            total += hidden * hidden
            blocks.append((hidden * table[z : z + 1]).astype(BF16))
        rows.append(jnp.concatenate(blocks, axis=1))
        squares.append(to_row(jnp.sum(total, axis=1, keepdims=True)))
    return jnp.concatenate(rows, axis=0), jnp.concatenate(squares, axis=0)


def head_block(own_ref, swapped_ref, start, pair):
    rows = pl.ds(pl.multiple_of(start, 128), 128)
    parts = [
        own_ref[...] if k == 0 else swapped_ref[k - 1, :, rows, :]
        for k in (2 * pair, 2 * pair + 1)
    ]
    return jnp.concatenate([part.reshape(NZ * 128, 128) for part in parts], axis=1)


def fetch_own(head_ref, x, start, block_ref, semaphore):
    rows = pl.ds(pl.multiple_of(start, 128), 128)
    fetch = pltpu.make_async_copy(head_ref.at[:, x, rows], block_ref, semaphore)
    fetch.start()
    return fetch


def near_kernel(mine_ref, gains_ref, head_ref, swapped_ref, out_ref, squares_ref, block_ref, semaphore):
    core = lax.axis_index("c")
    start = core * 128
    fetch = fetch_own(head_ref, x_index(), start, block_ref, semaphore)
    mine, squares_ref[...] = scaled_rows(mine_ref, gains_ref, core)
    fetch.wait()
    for pair in range(NX // 2):
        out_ref[pair] = jnp.dot(
            mine, head_block(block_ref, swapped_ref, start, pair), preferred_element_type=F32
        )


def far_kernel(
    other_ref, gains_ref, near_ref, squares_ref, head_ref, swapped_ref, out_ref, block_ref, semaphore
):
    x, core = x_index(), 1 - lax.axis_index("c")
    start = core * 128
    fetch = fetch_own(head_ref, x, start, block_ref, semaphore)
    other, squares = scaled_rows(other_ref, gains_ref, core)
    stats = jnp.concatenate(split_pair(squares + squares_ref[...]), axis=0).astype(BF16)
    fetch.wait()
    for pair in range(NX // 2):
        partial = near_ref[pair] + jnp.dot(
            other, head_block(block_ref, swapped_ref, start, pair), preferred_element_type=F32
        )
        partial = partial.astype(BF16)
        for k in range(2):
            target = lax.rem(x + NX - (2 * pair + k), NX)
            out_ref[target, 0:ROWS, :] = partial[:, 128 * k : 128 * k + 128]
            out_ref[target, ROWS : ROWS + 16, :] = stats


def logit_kernel(parts_ref, logits_ref, out_ref):
    stats = parts_ref[0, ROWS : ROWS + 16, :].astype(F32)
    for source in range(1, NX):
        stats += parts_ref[source, ROWS : ROWS + 16, :].astype(F32)
    factor = lax.rsqrt((stats[0:NY] + stats[NY:]) / D + 1e-05)
    masses = []
    for block in range(4):
        rows = slice(128 * block, 128 * block + 128)
        logits = parts_ref[0, rows, :].astype(F32)
        for source in range(1, NX):
            logits += parts_ref[source, rows, :].astype(F32)
        column = jnp.concatenate(
            [to_column(factor[2 * block + k : 2 * block + k + 1])[0:64] for k in range(2)], axis=0
        )
        logits = logits * column
        logits_ref[rows, :] = logits
        top = jnp.max(logits, axis=1, keepdims=True)
        total = jnp.sum(jnp.exp(logits - top), axis=1, keepdims=True)
        masses.append(to_row(top + jnp.log(total)))
    packed = jnp.concatenate(masses, axis=0)
    for target in range(NY * NC):
        out_ref[target] = packed


def merge_masses(masses):
    top = jnp.max(masses, axis=0)
    return top + jnp.log(jnp.sum(jnp.exp(masses - top[None]), axis=0))


def merge_kernel(parts_ref, out_ref):
    merged = merge_masses(parts_ref[...])
    for target in range(NZ * NX):
        out_ref[target] = merged


def vote_kernel(parts_ref, logits_ref, noise_ref, out_ref):
    merged = merge_masses(parts_ref[...])
    averaged = jnp.zeros((QUERIES, 128), F32)
    for block in range(4):
        mass = jnp.exp(
            logits_ref[128 * block : 128 * block + 128, :] - to_column(merged[block : block + 1])
        )
        averaged += jnp.sum(mass.reshape(8, QUERIES, 128), axis=0)
    out_ref[...] = jnp.log(VOCAB * (averaged / PROMPTS)) + noise_ref[...]


def shift(array, axis, step):
    count = lax.axis_size(axis)
    return lax.ppermute(array, axis, [(i, (i + step) % count) for i in range(count)])


def exchange(array, axes):
    return lax.all_to_all(array, axes, 0, 0, tiled=True)


def on_device(query, new_kv, cache, lengths, w_out, resid, norm_gain, head, noise):
    y, c = lax.axis_index("y"), lax.axis_index("c")
    x = x_index()
    blocks = head.reshape(NZ, NX, 256, 128)
    swapped = [
        shift(lax.dynamic_index_in_dim(blocks, (x + k) % NX, 1, keepdims=False), X, k)
        for k in range(1, NX)
    ]
    resid_mine = jnp.swapaxes(
        lax.dynamic_slice(resid, (0, 4 * y, 128 * c), (QUERIES, 4, 128)), 0, 1
    ).reshape(64, 128)

    other_w = shift(w_out, "near", 1)
    parts = call(
        attend_kernel,
        shape((NY * NC, 80, 128)),
        (lengths, query[:, 0, :], new_kv[:, :, 0, :], cache[:, 0]),
        "saaa",
        (
            pltpu.VMEM((QUERIES, D), BF16),
            pltpu.VMEM((2, QUERIES, KVH * HD), BF16),
            pltpu.VMEM((2, CACHE_ROWS, KVH * HD), BF16),
            pltpu.SemaphoreType.DMA((3,)),
        ),
        60,
    )
    parts = exchange(parts, ("c", "y"))
    attended = call(
        combine_kernel,
        shape((2 * NZ, 80, 128)),
        (parts, norm_gain.reshape(NC, 128), other_w),
        "vvw",
    )
    attended = exchange(attended, ("far", "z"))
    partial, gains = call(
        project_kernel,
        (shape((2 * NC * NY, 32, 128)), shape((NC, NZ, 128), F32)),
        (attended, w_out, other_w),
    )
    partial = exchange(partial, ("near", "c", "y"))
    hidden = call(
        residual_kernel,
        shape((NZ * NY, 64, 128)),
        (partial, resid_mine, swapped[1]),
        "vvw",
    )
    mine = exchange(hidden, ("y", "z"))
    mine, swapped = lax.optimization_barrier((mine, jnp.stack(swapped)))
    other = shift(mine, "c", 1)
    scratch = (pltpu.VMEM((NZ, 128, 128), BF16), pltpu.SemaphoreType.DMA)
    near, squares = call(
        near_kernel,
        (shape((NX // 2, ROWS, 256), F32), shape((NY, 128), F32)),
        (mine, gains, blocks, swapped),
        "vvav",
        scratch,
        12,
    )
    logits = call(
        far_kernel,
        shape((NX, ROWS + 16, 128)),
        (other, gains, near, squares, blocks, swapped),
        "vvvvav",
        scratch,
        12,
    )
    logits = exchange(logits, X)
    logits, stats = call(
        logit_kernel, (shape((ROWS, 128), F32), shape((NY * NC, 4, 128), F32)), (logits,)
    )
    stats = exchange(stats, ("c", "y"))
    stats = call(merge_kernel, shape((NZ * NX, 4, 128), F32), (stats,))
    stats = exchange(stats, X + ("z",))
    return call(vote_kernel, shape((QUERIES, 128), F32), (stats, logits, noise))


def solution(mesh):
    torus = Mesh(mesh.devices.reshape(NZ, 2, 2, NY, NC), MEMBER + TENSOR)
    placed = (
        P(None, MEMBER, None),
        P(None, None, MEMBER, None),
        P(None, MEMBER, TENSOR, None),
        P(MEMBER),
        P(TENSOR, MEMBER),
        P(None, None, MEMBER),
        P(MEMBER),
        P(None, MEMBER + TENSOR),
        P(None, MEMBER + TENSOR),
    )
    return jax.shard_map(
        on_device,
        mesh=torus,
        in_specs=placed,
        out_specs=P(None, MEMBER + TENSOR),
        check_vma=False,
    )
```
